512 devices in a mesh: replica: 8 (over z), fsdp: 8 (over x, core), tensor: 8 (over y).
Axes of the slice: x: 4, y: 8, z: 8, core: 2. Of those that a mesh axis runs over, the one named last changes fastest.
Arguments:
- momentum: bfloat16 [8, 4096, 14336], P('replica', 'fsdp', 'tensor'), may hold values from -64 to 64
- q_prev: bfloat16 [14336, 128], P('tensor'), may hold values from -4 to 4
Outputs:
- momentum_next: bfloat16 [8, 4096, 14336], P('replica', 'fsdp', 'tensor')
- update_left: float32 [4096, 128], P('fsdp')
- q_next: bfloat16 [14336, 128], P('tensor')
The draws below stay inside these ranges and needn't reach their ends.
All inputs are finite; a program needn't handle non-finite values.
Results may differ from the reference program's by a relative error of at most 0.02.
Values may be sent and summed in bfloat16 or wider, within the bound.
A program may use at most 64 MiB of HBM per device.

```python
import math
import jax
import jax.numpy as jnp
from jax import lax

D = 4096
FF = 14336
R = 128
ITERS = 3
REPLICAS = 8
N_REPLICA = 8


def draw_momentum(key, part):
    key = jax.random.fold_in(key, 11)
    keys = jax.random.split(key, 3)
    rows_scale = jnp.exp(jax.random.uniform(keys[0], (D,), jnp.float32) * math.log(10.0))
    cols_scale = jnp.exp(jax.random.uniform(keys[1], (FF,), jnp.float32) * math.log(10.0))
    row_pos = jnp.arange(D, dtype=jnp.float32) / (D - 1)
    col_pos = jnp.arange(FF, dtype=jnp.float32) / (FF - 1)
    noise = jnp.clip(jax.random.normal(keys[2], (REPLICAS, D, FF), jnp.float32), -4.0, 4.0)
    row_ramp = 1.0 + 0.7320508 * row_pos
    col_ramp = 1.0 + 0.7320508 * col_pos
    value = noise * (rows_scale * row_ramp)[None, :, None] * (cols_scale * col_ramp / 40.0)[None, None, :]
    return value.astype(jnp.bfloat16)


def shard_levels(rng, extent, cuts, least, largest):
    factor_of = 1.0
    for axis_at, blocks in cuts:
        draws = jax.random.uniform(jax.random.fold_in(jax.random.fold_in(rng, 6), axis_at), (blocks,), jnp.float32, least / len(cuts), largest / len(cuts))
        factor_of = factor_of * jnp.repeat(jnp.exp(draws), extent[axis_at] // blocks).reshape((-1,) + (1,) * (len(extent) - 1 - axis_at))
    return factor_of


def gaussian(own_key, shape, scale, limit, cuts=(), held_as=jnp.bfloat16):
    level = shard_levels(own_key, shape, cuts, -0.22, 0.18) if cuts else 1.0
    entries = jax.random.normal(own_key, shape, jnp.float32) * scale * level
    return jnp.minimum(jnp.maximum(entries, -limit), limit).astype(held_as)


def setup_inputs(seed: int = 0) -> dict:
    splits = jax.random.split(jax.random.key(seed), 3)
    momentum = draw_momentum(jax.random.fold_in(splits[2], 71), 0)
    q_prev = gaussian(splits[1], (FF, R), 1.0, 4.0, ((0, 8),))
    return {"momentum": momentum, "q_prev": q_prev}


ridge_scale = 1e-06
norm_eps = 1e-06
momentum_decay = 0.95

def orthonormal(rows, gram_total):
    rank = gram_total.shape[0]
    ridge = ridge_scale * jnp.trace(gram_total) / rank
    lower_factor = jnp.linalg.cholesky(gram_total + ridge * jnp.eye(rank, dtype=jnp.float32))
    return lax.linalg.triangular_solve(lower_factor, rows, left_side=False, lower=True, transpose_a=True)

def reference(momentum, q_prev):
    total = jnp.zeros((D, FF), jnp.float32)
    for index in range(N_REPLICA):
        total = total + momentum[index].astype(jnp.float32)
    mean_block = total / N_REPLICA
    factor_round = q_prev
    for iteration in range(ITERS):
        left_total = jnp.dot(mean_block, factor_round.astype(jnp.float32), precision=lax.Precision.HIGHEST)
        gram_total = jnp.dot(left_total.T, left_total, precision=lax.Precision.HIGHEST)
        left_round = orthonormal(left_total, gram_total).astype(jnp.bfloat16)
        right_total = jnp.dot(mean_block.T, left_round.astype(jnp.float32), precision=lax.Precision.HIGHEST)
        column_sq = lax.optimization_barrier(jnp.sum(right_total * right_total, axis=0))
        factor_round = (math.sqrt(FF) * right_total / jnp.sqrt(column_sq + norm_eps)).astype(jnp.bfloat16)
    right_round = right_total.astype(jnp.bfloat16)
    correction = jnp.dot(left_round.astype(jnp.float32), right_round.T.astype(jnp.float32), preferred_element_type=jnp.float32)
    momentum_next = jnp.stack([(momentum[index].astype(jnp.float32) - (1.0 - momentum_decay) * correction).astype(jnp.bfloat16) for index in range(N_REPLICA)])
    update_left = math.sqrt(D) * left_round.astype(jnp.float32)
    return (momentum_next, update_left, factor_round)
```

```python
import functools
import math

import jax
import jax.numpy as jnp
from jax import lax
from jax.experimental import pallas as pl
from jax.experimental.pallas import tpu as pltpu
from jax.sharding import PartitionSpec as P

D = 4096
FF = 14336
R = 128
ITERS = 3
NY, NZ, NX = 8, 8, 4
ROWS = 512
COLS = 1792
LY = ROWS // NY
RC = COLS // 2
RZ = RC // NZ

ridge_scale = 1e-06
norm_eps = 1e-06
momentum_decay = 0.95

MESH = pl.DeviceIdType.MESH
f32, bf16 = jnp.float32, jnp.bfloat16
HIGHEST = lax.Precision.HIGHEST


def split3(w):
    high = w.astype(bf16).astype(f32)
    rest = w - high
    mid = rest.astype(bf16).astype(f32)
    return high, mid, rest - mid


def factor_inverse(work):
    size = 16
    sub = lax.broadcasted_iota(jnp.int32, (size, R), 0)
    lane = lax.broadcasted_iota(jnp.int32, (size, R), 1)
    for first in range(0, R, size):
        left, right = work[first : first + size, 0:R], work[first : first + size, R : 2 * R]
        cols = [
            jnp.broadcast_to(left[:, first + k : first + k + 1], (size, R)) for k in range(size)
        ]
        scale = jnp.zeros((size, R), f32)
        for j in range(size):
            pivot = jnp.broadcast_to(cols[j][j : j + 1, :], (size, R))
            scale = jnp.where(sub == j, lax.rsqrt(pivot), scale)
            if j < size - 1:
                ratio = jnp.where(sub > j, cols[j], 0.0) * (1.0 / pivot)
                for k in range(j + 1, size):
                    cols[k] = cols[k] - ratio * cols[k][j : j + 1, :]
                left = left - ratio * left[j : j + 1, :]
                right = right - ratio * right[j : j + 1, :]
        left = jnp.where(lane >= first, left * scale, 0.0)
        right = right * scale
        work[first : first + size, 0:R] = left
        work[first : first + size, R : 2 * R] = right
        below = first + size
        if below < R:
            ph, pm, pw = split3(jnp.concatenate([left, right], 1))
            wh, wm, ww = split3(jnp.where(lane >= below, left, 0.0))
            a = jnp.concatenate([wh, wh, wm, wm, wh, ww], 0).astype(bf16)
            b = jnp.concatenate([ph, pm, ph, pm, pw, ph], 0).astype(bf16)
            update = lax.dot_general(a, b, (((0,), (0,)), ((), ())), preferred_element_type=f32)
            work[below:R, :] = work[below:R, :] - update[below:R, :]


def iterate_kernel(
    m_hbm, q_ref, lr_ref, rr_ref, d_ref,
    m, f, ls, ly, lz, la, gc, gx, gs, work, rcs, rc, rzs, rz, rx, ra, cs, scale,
    m_sem, ly_s, ly_r, lz_s, lz_r, la_s, la_r, gc_s, gc_r, gx_s, gx_r,
    rc_s, rc_r, rz_s, rz_r, rx_s, rx_r, ra_s, ra_r, rm_s, rm_r, cs_s, cs_r,
):
    z, fs, y = lax.axis_index("replica"), lax.axis_index("fsdp"), lax.axis_index("tensor")
    x, c = fs // 2, lax.rem(fs, 2)
    mate = {"fsdp": x * 2 + 1 - c}

    def at_y(k):
        return {"tensor": lax.rem(y + k, NY)}

    def at_z(k):
        return {"replica": lax.rem(z + k, NZ)}

    def at_x(k):
        return {"fsdp": lax.rem(x + k, NX) * 2 + c}

    def copy(src, dst, send, recv, to):
        return pltpu.make_async_remote_copy(
            src_ref=src, dst_ref=dst, send_sem=send, recv_sem=recv, device_id=to, device_id_type=MESH
        )

    load = pltpu.make_async_copy(m_hbm, m, m_sem)
    load.start()
    barrier = pltpu.get_barrier_semaphore()
    for k in range(1, NY):
        pl.semaphore_signal(barrier, inc=1, device_id=at_y(k), device_id_type=MESH)
    for k in range(1, NZ):
        pl.semaphore_signal(barrier, inc=1, device_id=at_z(k), device_id_type=MESH)
    for k in range(1, NX):
        pl.semaphore_signal(barrier, inc=1, device_id=at_x(k), device_id_type=MESH)
    pl.semaphore_signal(barrier, inc=1, device_id=mate, device_id_type=MESH)
    f[...] = q_ref[...]
    scale[...] = jnp.full((8, R), 1.0 / NZ, f32)
    load.wait()
    pl.semaphore_wait(barrier, NY + NZ + NX - 2)

    def column_scale(it):
        for k in range(1, NY):
            s = lax.rem(y + k, NY)
            copy(cs.at[it, s], cs.at[it, s], cs_s.at[k], cs_r.at[it, s], at_y(k)).wait_recv()
        total = cs[it, 0]
        for s in range(1, NY):
            total = total + cs[it, s]
        scale[...] = math.sqrt(FF) / jnp.sqrt(total + norm_eps)

    def iteration(it, carry):
        ls[...] = jnp.dot(m[...], f[...], preferred_element_type=f32).astype(bf16)
        sends = []

        def start(cp):
            cp.start()
            sends.append(cp)

        for k in range(1, NY):
            t = lax.rem(y + k, NY)
            start(copy(ls.at[pl.ds(t * LY, LY)], ly.at[it, y], ly_s.at[k], ly_r.at[it, y], at_y(k)))
        total = ls[pl.ds(y * LY, LY), :].astype(f32)
        for k in range(1, NY):
            s = lax.rem(y + k, NY)
            copy(ly.at[it, s], ly.at[it, s], ly_s.at[k], ly_r.at[it, s], at_y(k)).wait_recv()
            total = total + ly[it, s].astype(f32)
        lz[it, z] = total.astype(bf16)
        for k in range(1, NZ):
            start(copy(lz.at[it, z], lz.at[it, z], lz_s.at[k], lz_r.at[it, z], at_z(k)))

        @pl.when(it > 0)
        def _():
            column_scale(it - 1)
            scale[...] = scale[...] * (1.0 / NZ)

        for k in range(1, NZ):
            s = lax.rem(z + k, NZ)
            copy(lz.at[it, s], lz.at[it, s], lz_s.at[k], lz_r.at[it, s], at_z(k)).wait_recv()
        total = lz[it, 0].astype(f32)
        for s in range(1, NZ):
            total = total + lz[it, s].astype(f32)
        la[it, pl.ds(y * LY, LY), :] = (total * scale[0:1, :]).astype(bf16)
        mine = la.at[it, pl.ds(y * LY, LY)]
        for k in range(1, NY):
            start(copy(mine, mine, la_s.at[k], la_r.at[it, y], at_y(k)))
        for k in range(1, NY):
            s = lax.rem(y + k, NY)
            theirs = la.at[it, pl.ds(s * LY, LY)]
            copy(theirs, theirs, la_s.at[k], la_r.at[it, s], at_y(k)).wait_recv()
        left = la[it]

        def product(half):
            columns = pl.ds(pl.multiple_of(half * RC, 128), RC)
            return lax.dot_general(
                m[:, columns], left, (((0,), (0,)), ((), ())), preferred_element_type=f32
            )

        gs[...] = lax.dot_general(left, left, (((0,), (0,)), ((), ())), preferred_element_type=f32)
        to_gram = copy(gs, gc.at[it], gc_s, gc_r.at[it], mate)
        start(to_gram)
        rcs[...] = product(1 - c)
        to_mate = copy(rcs, rc.at[it], rc_s, rc_r.at[it], mate)
        start(to_mate)
        own = product(c)
        to_gram.wait_recv()
        gx[it, x] = gs[...] + gc[it]
        for k in range(1, NX):
            start(copy(gx.at[it, x], gx.at[it, x], gx_s.at[k], gx_r.at[it, x], at_x(k)))
        to_mate.wait_recv()
        rzs[...] = (own + rc[it]).astype(bf16)
        for k in range(1, NZ):
            t = lax.rem(z + k, NZ)
            start(copy(rzs.at[pl.ds(t * RZ, RZ)], rz.at[it, z], rz_s.at[k], rz_r.at[it, z], at_z(k)))

        for k in range(1, NX):
            s = lax.rem(x + k, NX)
            copy(gx.at[it, s], gx.at[it, s], gx_s.at[k], gx_r.at[it, s], at_x(k)).wait_recv()
        gram = (gx[it, 0] + gx[it, 1]) + (gx[it, 2] + gx[it, 3])
        eye = lax.broadcasted_iota(jnp.int32, (R, R), 0) == lax.broadcasted_iota(
            jnp.int32, (R, R), 1
        )
        ridge = (ridge_scale / R) * jnp.sum(jnp.where(eye, gram, 0.0), keepdims=True)
        work[:, 0:R] = jnp.where(eye, gram + ridge, gram)
        work[:, R : 2 * R] = jnp.where(eye, 1.0, 0.0)
        factor_inverse(work)

        total = rzs[pl.ds(z * RZ, RZ), :].astype(f32)
        for k in range(1, NZ):
            s = lax.rem(z + k, NZ)
            copy(rz.at[it, s], rz.at[it, s], rz_s.at[k], rz_r.at[it, s], at_z(k)).wait_recv()
            total = total + rz[it, s].astype(f32)
        rx[it, x] = total.astype(bf16)
        for k in range(1, NX):
            start(copy(rx.at[it, x], rx.at[it, x], rx_s.at[k], rx_r.at[it, x], at_x(k)))
        for k in range(1, NX):
            s = lax.rem(x + k, NX)
            copy(rx.at[it, s], rx.at[it, s], rx_s.at[k], rx_r.at[it, s], at_x(k)).wait_recv()
        total = (rx[it, 0].astype(f32) + rx[it, 1].astype(f32)) + (
            rx[it, 2].astype(f32) + rx[it, 3].astype(f32)
        )
        right = lax.dot_general(
            total, work[:, R : 2 * R], (((1,), (1,)), ((), ())),
            preferred_element_type=f32, precision=HIGHEST,
        )
        here = c * RC + z * RZ
        ra[it, pl.ds(here, RZ), :] = (right * (1.0 / NZ)).astype(bf16)
        mine = ra.at[it, pl.ds(here, RZ)]
        for k in range(1, NZ):
            start(copy(mine, mine, ra_s.at[k], ra_r.at[it, z], at_z(k)))
        start(copy(mine, mine, rm_s.at[0], rm_r.at[it, z], mate))
        for k in range(1, NZ):
            s = lax.rem(z + k, NZ)
            theirs = ra.at[it, pl.ds(c * RC + s * RZ, RZ)]
            copy(theirs, theirs, ra_s.at[k], ra_r.at[it, s], at_z(k)).wait_recv()
            start(copy(theirs, theirs, rm_s.at[k], rm_r.at[it, s], mate))
        for k in range(NZ):
            s = lax.rem(z + k, NZ)
            theirs = ra.at[it, pl.ds((1 - c) * RC + s * RZ, RZ)]
            copy(theirs, theirs, rm_s.at[k], rm_r.at[it, s], mate).wait_recv()
        factor = ra[it]
        f[...] = factor
        wide = factor.astype(f32)
        cs[it, y] = jnp.broadcast_to(jnp.sum(wide * wide, axis=0, keepdims=True), (8, R))
        for k in range(1, NY):
            start(copy(cs.at[it, y], cs.at[it, y], cs_s.at[k], cs_r.at[it, y], at_y(k)))
        for cp in sends:
            cp.wait_send()
        return carry

    lax.fori_loop(0, ITERS, iteration, 0)
    last = ITERS - 1
    lr_ref[...] = lax.dot_general(
        la[last].astype(f32), work[:, R : 2 * R], (((1,), (1,)), ((), ())),
        preferred_element_type=f32, precision=HIGHEST,
    ).astype(bf16)
    rr_ref[...] = f[...]
    column_scale(last)
    d_ref[...] = scale[...]


def iterate(block, q):
    vmem = pl.BlockSpec(memory_space=pltpu.VMEM)
    dma = pltpu.SemaphoreType.DMA
    n = ITERS
    return pl.pallas_call(
        iterate_kernel,
        out_shape=[
            jax.ShapeDtypeStruct((ROWS, R), bf16),
            jax.ShapeDtypeStruct((COLS, R), bf16),
            jax.ShapeDtypeStruct((8, R), f32),
        ],
        in_specs=[pl.BlockSpec(memory_space=pl.ANY), vmem],
        out_specs=[vmem] * 3,
        scratch_shapes=[
            pltpu.VMEM((ROWS, COLS), bf16),
            pltpu.VMEM((COLS, R), bf16),
            pltpu.VMEM((ROWS, R), bf16),
            pltpu.VMEM((n, NY, LY, R), bf16),
            pltpu.VMEM((n, NZ, LY, R), bf16),
            pltpu.VMEM((n, ROWS, R), bf16),
            pltpu.VMEM((n, R, R), f32),
            pltpu.VMEM((n, NX, R, R), f32),
            pltpu.VMEM((R, R), f32),
            pltpu.VMEM((R, 2 * R), f32),
            pltpu.VMEM((RC, R), f32),
            pltpu.VMEM((n, RC, R), f32),
            pltpu.VMEM((RC, R), bf16),
            pltpu.VMEM((n, NZ, RZ, R), bf16),
            pltpu.VMEM((n, NX, RZ, R), bf16),
            pltpu.VMEM((n, COLS, R), bf16),
            pltpu.VMEM((n, NY, 8, R), f32),
            pltpu.VMEM((8, R), f32),
            dma(()),
            dma((NY,)), dma((n, NY)),
            dma((NZ,)), dma((n, NZ)),
            dma((NY,)), dma((n, NY)),
            dma(()), dma((n,)),
            dma((NX,)), dma((n, NX)),
            dma(()), dma((n,)),
            dma((NZ,)), dma((n, NZ)),
            dma((NX,)), dma((n, NX)),
            dma((NZ,)), dma((n, NZ)),
            dma((NZ,)), dma((n, NZ)),
            dma((NY,)), dma((n, NY)),
        ],
        compiler_params=pltpu.CompilerParams(
            collective_id=0, has_side_effects=True, vmem_limit_bytes=40 << 20
        ),
        cost_estimate=pl.CostEstimate(
            flops=12 * ROWS * COLS * R, bytes_accessed=2 * ROWS * COLS, transcendentals=0
        ),
    )(block, q)


def finish_kernel(m, left, right, scale, m_out, u_out, q_out):
    correction = lax.dot_general(
        left[...], right[...], (((1,), (1,)), ((), ())), preferred_element_type=f32
    )
    m_out[...] = (m[...].astype(f32) - (1.0 - momentum_decay) * correction).astype(bf16)
    u_out[...] = math.sqrt(D) * left[...].astype(f32)

    @pl.when(pl.program_id(0) == 0)
    def _():
        q_out[...] = (right[...].astype(f32) * scale[0:1, :]).astype(bf16)


def finish(block, left, right, scale):
    steps = 4
    rows = ROWS // steps
    return pl.pallas_call(
        finish_kernel,
        grid=(steps,),
        out_shape=[
            jax.ShapeDtypeStruct((ROWS, COLS), bf16),
            jax.ShapeDtypeStruct((ROWS, R), f32),
            jax.ShapeDtypeStruct((COLS, R), bf16),
        ],
        in_specs=[
            pl.BlockSpec((rows, COLS), lambda i: (i, 0)),
            pl.BlockSpec((rows, R), lambda i: (i, 0)),
            pl.BlockSpec((COLS, R), lambda i: (0, 0)),
            pl.BlockSpec((8, R), lambda i: (0, 0)),
        ],
        out_specs=[
            pl.BlockSpec((rows, COLS), lambda i: (i, 0)),
            pl.BlockSpec((rows, R), lambda i: (i, 0)),
            pl.BlockSpec((COLS, R), lambda i: (0, 0)),
        ],
        compiler_params=pltpu.CompilerParams(vmem_limit_bytes=40 << 20),
        cost_estimate=pl.CostEstimate(
            flops=2 * ROWS * COLS * R, bytes_accessed=4 * ROWS * COLS, transcendentals=0
        ),
    )(block, left, right, scale)


def shards(momentum, q_prev):
    block = momentum[0]
    left, right, scale = iterate(block, q_prev)
    momentum_next, update_left, q_next = finish(block, left, right, scale)
    return momentum_next[None], update_left, q_next


def solution(mesh):
    in_specs = (P("replica", "fsdp", "tensor"), P("tensor", None))
    out_specs = (P("replica", "fsdp", "tensor"), P("fsdp", None), P("tensor", None))
    return jax.shard_map(shards, mesh=mesh, in_specs=in_specs, out_specs=out_specs, check_vma=False)
```

```python
import functools
import math

import jax
import jax.numpy as jnp
from jax import lax
from jax.experimental import pallas as pl
from jax.experimental.pallas import tpu as pltpu
from jax.sharding import PartitionSpec as P

D = 4096
FF = 14336
R = 128
ITERS = 3
NY, NZ, NX = 8, 8, 4
ROWS = 512
COLS = 1792
LY = ROWS // NY
LZ = ROWS // NZ
HZ = LZ // 2
RC = COLS // 2
RZ = RC // NZ

ridge_scale = 1e-06
norm_eps = 1e-06
momentum_decay = 0.95

MESH = pl.DeviceIdType.MESH
f32, bf16 = jnp.float32, jnp.bfloat16
HIGHEST = lax.Precision.HIGHEST


def split3(w):
    high = w.astype(bf16).astype(f32)
    rest = w - high
    mid = rest.astype(bf16).astype(f32)
    return high, mid, rest - mid


def factor_inverse(work):
    size = 16
    sub = lax.broadcasted_iota(jnp.int32, (size, R), 0)
    lane = lax.broadcasted_iota(jnp.int32, (size, R), 1)
    for first in range(0, R, size):
        left, right = work[first : first + size, 0:R], work[first : first + size, R : 2 * R]
        cols = [
            jnp.broadcast_to(left[:, first + k : first + k + 1], (size, R)) for k in range(size)
        ]
        scale = jnp.zeros((size, R), f32)
        for j in range(size):
            pivot = jnp.broadcast_to(cols[j][j : j + 1, :], (size, R))
            scale = jnp.where(sub == j, lax.rsqrt(pivot), scale)
            if j < size - 1:
                ratio = jnp.where(sub > j, cols[j], 0.0) * (1.0 / pivot)
                for k in range(j + 1, size):
                    cols[k] = cols[k] - ratio * cols[k][j : j + 1, :]
                left = left - ratio * left[j : j + 1, :]
                right = right - ratio * right[j : j + 1, :]
        left = jnp.where(lane >= first, left * scale, 0.0)
        right = right * scale
        work[first : first + size, 0:R] = left
        work[first : first + size, R : 2 * R] = right
        below = first + size
        if below < R:
            ph, pm, pw = split3(jnp.concatenate([left, right], 1))
            wh, wm, ww = split3(jnp.where(lane >= below, left, 0.0))
            a = jnp.concatenate([wh, wh, wm, wm, wh, ww], 0).astype(bf16)
            b = jnp.concatenate([ph, pm, ph, pm, pw, ph], 0).astype(bf16)
            update = lax.dot_general(a, b, (((0,), (0,)), ((), ())), preferred_element_type=f32)
            work[below:R, :] = work[below:R, :] - update[below:R, :]


def iterate_kernel(
    m_hbm, q_hbm, lr_ref, rr_ref, d_ref,
    m, f, ms, ring, ls, ly, lz, la, gc, gx, gs, work, rcs, rc, rzs, rz, rx, ra, cy, cz, cc, scale,
    m_sem, q_sem, ring_s, ring_r, ly_s, ly_r, lz_s, lz_r, la_s, la_r, gc_s, gc_r, gx_s, gx_r,
    rc_s, rc_r, rz_s, rz_r, rx_s, rx_r, ra_s, ra_r, rm_s, rm_r, cy_s, cy_r, cz_s, cz_r, cc_s, cc_r,
):
    z, fs, y = lax.axis_index("replica"), lax.axis_index("fsdp"), lax.axis_index("tensor")
    x, c = fs // 2, lax.rem(fs, 2)
    mate = {"fsdp": x * 2 + 1 - c}

    def at_y(k):
        return {"tensor": lax.rem(y + k, NY)}

    def at_z(k):
        return {"replica": lax.rem(z + k, NZ)}

    def at_x(k):
        return {"fsdp": lax.rem(x + k, NX) * 2 + c}

    def copy(src, dst, send, recv, to):
        return pltpu.make_async_remote_copy(
            src_ref=src, dst_ref=dst, send_sem=send, recv_sem=recv, device_id=to, device_id_type=MESH
        )

    load_m = pltpu.make_async_copy(m_hbm, m, m_sem)
    load_m.start()
    load_q = pltpu.make_async_copy(q_hbm, f, q_sem)
    load_q.start()
    barrier = pltpu.get_barrier_semaphore()
    for k in range(1, NY):
        pl.semaphore_signal(barrier, inc=1, device_id=at_y(k), device_id_type=MESH)
    for k in range(1, NZ):
        pl.semaphore_signal(barrier, inc=1, device_id=at_z(k), device_id_type=MESH)
    for k in range(1, NX):
        pl.semaphore_signal(barrier, inc=1, device_id=at_x(k), device_id_type=MESH)
    pl.semaphore_signal(barrier, inc=1, device_id=mate, device_id_type=MESH)
    scale[...] = jnp.full((8, R), 1.0 / NZ, f32)
    load_q.wait()
    load_m.wait()
    pl.semaphore_wait(barrier, NY + NZ + NX - 2)

    def chunk(way, j):
        return pl.ds(pl.multiple_of(lax.rem(j + 2 * NZ, NZ) * LZ + way * HZ, HZ), HZ)

    def ring_copy(way, step):
        step_to = 1 if way == 0 else NZ - 1
        if step == 1:
            src = m.at[chunk(way, z - 1 if way == 0 else z + 1)]
        else:
            src = ring.at[way, step - 2]
        return copy(src, ring.at[way, step - 1], ring_s.at[way, step - 1],
                    ring_r.at[way, step - 1], at_z(step_to))

    def ring_step(step):
        for way in range(2):
            if step > 1:
                ring_copy(way, step - 1).wait_recv()
                own = m[chunk(way, z - step if way == 0 else z + step), :].astype(f32)
                ring[way, step - 2] = (ring[way, step - 2].astype(f32) + own).astype(bf16)
            ring_copy(way, step).start()

    def ring_end():
        for way in range(2):
            ring_copy(way, NZ - 1).wait_recv()
            total = ring[way, NZ - 2].astype(f32) + m[chunk(way, z), :].astype(f32)
            high = total.astype(bf16)
            ms[way * HZ : (way + 1) * HZ, :] = high
            ms[LZ + way * HZ : LZ + (way + 1) * HZ, :] = (total - high.astype(f32)).astype(bf16)

    def sums_over_z(it):
        for k in range(1, NZ):
            s = lax.rem(z + k, NZ)
            copy(cz.at[it, s], cz.at[it, s], cz_s.at[k], cz_r.at[it, s], at_z(k)).wait_recv()
        total = cz[it, 0]
        for s in range(1, NZ):
            total = total + cz[it, s]
        cc[it, 0] = total
        copy(cc.at[it, 0], cc.at[it, 1], cc_s, cc_r.at[it], mate).start()

    def column_scale(it):
        copy(cc.at[it, 0], cc.at[it, 1], cc_s, cc_r.at[it], mate).wait()
        scale[...] = math.sqrt(FF) / jnp.sqrt(cc[it, 0] + cc[it, 1] + norm_eps)

    def left_first(it, start):
        ls[...] = jnp.dot(m[...], f[...], preferred_element_type=f32).astype(bf16)
        for k in range(1, NY):
            t = lax.rem(y + k, NY)
            start(copy(ls.at[pl.ds(t * LY, LY)], ly.at[it, y], ly_s.at[k], ly_r.at[it, y], at_y(k)))
        ring_step(1)
        total = ls[pl.ds(y * LY, LY), :].astype(f32)
        for k in range(1, NY):
            s = lax.rem(y + k, NY)
            copy(ly.at[it, s], ly.at[it, s], ly_s.at[k], ly_r.at[it, s], at_y(k)).wait_recv()
            total = total + ly[it, s].astype(f32)
        lz[z] = total.astype(bf16)
        for k in range(1, NZ):
            start(copy(lz.at[z], lz.at[z], lz_s.at[k], lz_r.at[z], at_z(k)))
        ring_step(2)
        for k in range(1, NZ):
            s = lax.rem(z + k, NZ)
            copy(lz.at[s], lz.at[s], lz_s.at[k], lz_r.at[s], at_z(k)).wait_recv()
        total = lz[0].astype(f32)
        for s in range(1, NZ):
            total = total + lz[s].astype(f32)
        la[it, pl.ds(y * LY, LY), :] = (total * scale[0:1, :]).astype(bf16)
        mine = la.at[it, pl.ds(y * LY, LY)]
        for k in range(1, NY):
            start(copy(mine, mine, la_s.at[k], la_r.at[it, y], at_y(k)))
        ring_step(3)
        for k in range(1, NY):
            s = lax.rem(y + k, NY)
            theirs = la.at[it, pl.ds(s * LY, LY)]
            copy(theirs, theirs, la_s.at[k], la_r.at[it, s], at_y(k)).wait_recv()

    def left_later(it, start):
        both = jnp.dot(ms[...], f[...], preferred_element_type=f32)
        ly[it, y] = (both[0:LZ, :] + both[LZ : 2 * LZ, :]).astype(bf16)
        for k in range(1, NY):
            start(copy(ly.at[it, y], ly.at[it, y], ly_s.at[k], ly_r.at[it, y], at_y(k)))
        sums_over_z(it - 1)
        for k in range(1, NY):
            s = lax.rem(y + k, NY)
            copy(ly.at[it, s], ly.at[it, s], ly_s.at[k], ly_r.at[it, s], at_y(k)).wait_recv()
        column_scale(it - 1)
        total = ly[it, 0].astype(f32)
        for s in range(1, NY):
            total = total + ly[it, s].astype(f32)
        rows = (total * (scale[0:1, :] * (1.0 / NZ))).astype(bf16)
        la[it, pl.ds(z * LZ, LZ), :] = rows
        mine = la.at[it, pl.ds(z * LZ, LZ)]
        for k in range(1, NZ):
            start(copy(mine, mine, la_s.at[k], la_r.at[it, z], at_z(k)))
        return rows

    def wait_left_later(it):
        for k in range(1, NZ):
            s = lax.rem(z + k, NZ)
            theirs = la.at[it, pl.ds(s * LZ, LZ)]
            copy(theirs, theirs, la_s.at[k], la_r.at[it, s], at_z(k)).wait_recv()

    def product(block, left, half):
        columns = pl.ds(pl.multiple_of(half * RC, 128), RC)
        return lax.dot_general(
            block[:, columns], left, (((0,), (0,)), ((), ())), preferred_element_type=f32
        )

    def iteration(it, first):
        sends = []

        def start(cp):
            cp.start()
            sends.append(cp)

        def gram_to_mate():
            left = la[it]
            gs[...] = lax.dot_general(
                left, left, (((0,), (0,)), ((), ())), preferred_element_type=f32
            )
            start(copy(gs, gc.at[it], gc_s, gc_r.at[it], mate))

        def gram_over_x():
            copy(gs, gc.at[it], gc_s, gc_r.at[it], mate).wait_recv()
            gx[it, x] = gs[...] + gc[it]
            for k in range(1, NX):
                start(copy(gx.at[it, x], gx.at[it, x], gx_s.at[k], gx_r.at[it, x], at_x(k)))

        if first:
            left_first(it, start)
            ring_step(4)
            gram_to_mate()
            block, rows = m, la[it]
        else:
            rows = left_later(it, start)
            block, rows = ms, jnp.concatenate([rows, rows], 0)
        rcs[...] = product(block, rows, 1 - c)
        to_mate = copy(rcs, rc.at[it], rc_s, rc_r.at[it], mate)
        start(to_mate)
        own = product(block, rows, c)
        if first:
            gram_over_x()
        to_mate.wait_recv()
        rzs[...] = (own + rc[it]).astype(bf16)
        for k in range(1, NZ):
            t = lax.rem(z + k, NZ)
            start(copy(rzs.at[pl.ds(t * RZ, RZ)], rz.at[it, z], rz_s.at[k], rz_r.at[it, z], at_z(k)))
        if not first:
            wait_left_later(it)
            gram_to_mate()
            gram_over_x()

        for k in range(1, NX):
            s = lax.rem(x + k, NX)
            copy(gx.at[it, s], gx.at[it, s], gx_s.at[k], gx_r.at[it, s], at_x(k)).wait_recv()
        if first:
            ring_step(5)
        gram = (gx[it, 0] + gx[it, 1]) + (gx[it, 2] + gx[it, 3])
        eye = lax.broadcasted_iota(jnp.int32, (R, R), 0) == lax.broadcasted_iota(
            jnp.int32, (R, R), 1
        )
        ridge = (ridge_scale / R) * jnp.sum(jnp.where(eye, gram, 0.0), keepdims=True)
        work[:, 0:R] = jnp.where(eye, gram + ridge, gram)
        work[:, R : 2 * R] = jnp.where(eye, 1.0, 0.0)
        factor_inverse(work)

        total = rzs[pl.ds(z * RZ, RZ), :].astype(f32)
        for k in range(1, NZ):
            s = lax.rem(z + k, NZ)
            copy(rz.at[it, s], rz.at[it, s], rz_s.at[k], rz_r.at[it, s], at_z(k)).wait_recv()
            total = total + rz[it, s].astype(f32)
        rx[it, x] = total.astype(bf16)
        for k in range(1, NX):
            start(copy(rx.at[it, x], rx.at[it, x], rx_s.at[k], rx_r.at[it, x], at_x(k)))
        if first:
            ring_step(6)
        for k in range(1, NX):
            s = lax.rem(x + k, NX)
            copy(rx.at[it, s], rx.at[it, s], rx_s.at[k], rx_r.at[it, s], at_x(k)).wait_recv()
        total = (rx[it, 0].astype(f32) + rx[it, 1].astype(f32)) + (
            rx[it, 2].astype(f32) + rx[it, 3].astype(f32)
        )
        right = lax.dot_general(
            total, work[:, R : 2 * R], (((1,), (1,)), ((), ())),
            preferred_element_type=f32, precision=HIGHEST,
        ) * (1.0 / NZ)
        here = c * RC + z * RZ
        ra[it, pl.ds(here, RZ), :] = right.astype(bf16)
        mine = ra.at[it, pl.ds(here, RZ)]
        for k in range(1, NZ):
            start(copy(mine, mine, ra_s.at[k], ra_r.at[it, z], at_z(k)))
        cy[it, y] = jnp.broadcast_to(jnp.sum(right * right, axis=0, keepdims=True), (8, R))
        for k in range(1, NY):
            start(copy(cy.at[it, y], cy.at[it, y], cy_s.at[k], cy_r.at[it, y], at_y(k)))
        start(copy(mine, mine, rm_s.at[0], rm_r.at[it, z], mate))
        if first:
            ring_step(7)
        for k in range(1, NY):
            s = lax.rem(y + k, NY)
            copy(cy.at[it, s], cy.at[it, s], cy_s.at[k], cy_r.at[it, s], at_y(k)).wait_recv()
        total = cy[it, 0]
        for s in range(1, NY):
            total = total + cy[it, s]
        cz[it, z] = total
        for k in range(1, NZ):
            start(copy(cz.at[it, z], cz.at[it, z], cz_s.at[k], cz_r.at[it, z], at_z(k)))
        for k in (1, 7, 2, 6, 3, 5, 4):
            s = lax.rem(z + k, NZ)
            theirs = ra.at[it, pl.ds(c * RC + s * RZ, RZ)]
            copy(theirs, theirs, ra_s.at[k], ra_r.at[it, s], at_z(k)).wait_recv()
            start(copy(theirs, theirs, rm_s.at[k], rm_r.at[it, s], mate))
        if first:
            ring_end()
        for k in range(NZ):
            s = lax.rem(z + k, NZ)
            theirs = ra.at[it, pl.ds((1 - c) * RC + s * RZ, RZ)]
            copy(theirs, theirs, rm_s.at[k], rm_r.at[it, s], mate).wait_recv()
        f[...] = ra[it]
        for cp in sends:
            cp.wait_send()
        if first:
            for way in range(2):
                for step in range(1, NZ):
                    ring_copy(way, step).wait_send()

    iteration(0, True)

    def again(it, carry):
        iteration(it, False)
        return carry

    lax.fori_loop(1, ITERS, again, 0)
    last = ITERS - 1
    lr_ref[...] = lax.dot_general(
        la[last].astype(f32), work[:, R : 2 * R], (((1,), (1,)), ((), ())),
        preferred_element_type=f32, precision=HIGHEST,
    ).astype(bf16)
    rr_ref[...] = f[...]
    sums_over_z(last)
    column_scale(last)
    d_ref[...] = scale[...]


def iterate(block, q):
    vmem = pl.BlockSpec(memory_space=pltpu.VMEM)
    hbm = pl.BlockSpec(memory_space=pltpu.HBM)
    dma = pltpu.SemaphoreType.DMA
    n = ITERS
    return pl.pallas_call(
        iterate_kernel,
        out_shape=[
            jax.ShapeDtypeStruct((ROWS, R), bf16),
            jax.ShapeDtypeStruct((COLS, R), bf16),
            jax.ShapeDtypeStruct((8, R), f32),
        ],
        in_specs=[hbm, hbm],
        out_specs=[vmem] * 3,
        scratch_shapes=[
            pltpu.VMEM((ROWS, COLS), bf16),
            pltpu.VMEM((COLS, R), bf16),
            pltpu.VMEM((2 * LZ, COLS), bf16),
            pltpu.VMEM((2, NZ - 1, HZ, COLS), bf16),
            pltpu.VMEM((ROWS, R), bf16),
            pltpu.VMEM((n, NY, LY, R), bf16),
            pltpu.VMEM((NZ, LY, R), bf16),
            pltpu.VMEM((n, ROWS, R), bf16),
            pltpu.VMEM((n, R, R), f32),
            pltpu.VMEM((n, NX, R, R), f32),
            pltpu.VMEM((R, R), f32),
            pltpu.VMEM((R, 2 * R), f32),
            pltpu.VMEM((RC, R), f32),
            pltpu.VMEM((n, RC, R), f32),
            pltpu.VMEM((RC, R), bf16),
            pltpu.VMEM((n, NZ, RZ, R), bf16),
            pltpu.VMEM((n, NX, RZ, R), bf16),
            pltpu.VMEM((n, COLS, R), bf16),
            pltpu.VMEM((n, NY, 8, R), f32),
            pltpu.VMEM((n, NZ, 8, R), f32),
            pltpu.VMEM((n, 2, 8, R), f32),
            pltpu.VMEM((8, R), f32),
            dma(()), dma(()),
            dma((2, NZ - 1)), dma((2, NZ - 1)),
            dma((NY,)), dma((n, NY)),
            dma((NZ,)), dma((NZ,)),
            dma((NY,)), dma((n, NY)),
            dma(()), dma((n,)),
            dma((NX,)), dma((n, NX)),
            dma(()), dma((n,)),
            dma((NZ,)), dma((n, NZ)),
            dma((NX,)), dma((n, NX)),
            dma((NZ,)), dma((n, NZ)),
            dma((NZ,)), dma((n, NZ)),
            dma((NY,)), dma((n, NY)),
            dma((NZ,)), dma((n, NZ)),
            dma(()), dma((n,)),
        ],
        compiler_params=pltpu.CompilerParams(
            collective_id=0, has_side_effects=True, vmem_limit_bytes=56 << 20
        ),
        cost_estimate=pl.CostEstimate(
            flops=12 * ROWS * COLS * R, bytes_accessed=2 * ROWS * COLS, transcendentals=0
        ),
    )(block, q)


def finish_kernel(m, left, right, scale, m_out, u_out, q_out):
    correction = lax.dot_general(
        left[...], right[...], (((1,), (1,)), ((), ())), preferred_element_type=f32
    )
    m_out[...] = (m[...].astype(f32) - (1.0 - momentum_decay) * correction).astype(bf16)
    u_out[...] = math.sqrt(D) * left[...].astype(f32)

    @pl.when(pl.program_id(0) == 0)
    def _():
        q_out[...] = (right[...].astype(f32) * scale[0:1, :]).astype(bf16)


def finish(block, left, right, scale):
    steps = 4
    rows = ROWS // steps
    return pl.pallas_call(
        finish_kernel,
        grid=(steps,),
        out_shape=[
            jax.ShapeDtypeStruct((ROWS, COLS), bf16),
            jax.ShapeDtypeStruct((ROWS, R), f32),
            jax.ShapeDtypeStruct((COLS, R), bf16),
        ],
        in_specs=[
            pl.BlockSpec((rows, COLS), lambda i: (i, 0)),
            pl.BlockSpec((rows, R), lambda i: (i, 0)),
            pl.BlockSpec((COLS, R), lambda i: (0, 0)),
            pl.BlockSpec((8, R), lambda i: (0, 0)),
        ],
        out_specs=[
            pl.BlockSpec((rows, COLS), lambda i: (i, 0)),
            pl.BlockSpec((rows, R), lambda i: (i, 0)),
            pl.BlockSpec((COLS, R), lambda i: (0, 0)),
        ],
        compiler_params=pltpu.CompilerParams(vmem_limit_bytes=56 << 20),
        cost_estimate=pl.CostEstimate(
            flops=2 * ROWS * COLS * R, bytes_accessed=4 * ROWS * COLS, transcendentals=0
        ),
    )(block, left, right, scale)


def shards(momentum, q_prev):
    block = momentum[0]
    left, right, scale = iterate(block, q_prev)
    momentum_next, update_left, q_next = finish(block, left, right, scale)
    return momentum_next[None], update_left, q_next


def solution(mesh):
    in_specs = (P("replica", "fsdp", "tensor"), P("tensor", None))
    out_specs = (P("replica", "fsdp", "tensor"), P("fsdp", None), P("tensor", None))
    return jax.shard_map(shards, mesh=mesh, in_specs=in_specs, out_specs=out_specs, check_vma=False)
```

```python
import functools
import math

import jax
import jax.numpy as jnp
from jax import lax
from jax.experimental import pallas as pl
from jax.experimental.pallas import tpu as pltpu
from jax.sharding import PartitionSpec as P

D = 4096
FF = 14336
R = 128
ITERS = 3
NY, NZ, NX = 8, 8, 4
ROWS = 512
COLS = 1792
LY = ROWS // NY
LZ = ROWS // NZ
HZ = LZ // 2
RC = COLS // 2
RZ = RC // NZ
PARTS = ((0, 112),)

ridge_scale = 1e-06
norm_eps = 1e-06
momentum_decay = 0.95

MESH = pl.DeviceIdType.MESH
f32, bf16 = jnp.float32, jnp.bfloat16
HIGHEST = lax.Precision.HIGHEST


def split3(w):
    high = w.astype(bf16).astype(f32)
    rest = w - high
    mid = rest.astype(bf16).astype(f32)
    return high, mid, rest - mid


def factor_inverse(work):
    size = 16
    sub = lax.broadcasted_iota(jnp.int32, (size, R), 0)
    lane = lax.broadcasted_iota(jnp.int32, (size, R), 1)
    for first in range(0, R, size):
        left, right = work[first : first + size, 0:R], work[first : first + size, R : 2 * R]
        cols = [
            jnp.broadcast_to(left[:, first + k : first + k + 1], (size, R)) for k in range(size)
        ]
        scale = jnp.zeros((size, R), f32)
        for j in range(size):
            pivot = jnp.broadcast_to(cols[j][j : j + 1, :], (size, R))
            scale = jnp.where(sub == j, lax.rsqrt(pivot), scale)
            if j < size - 1:
                ratio = jnp.where(sub > j, cols[j], 0.0) * (1.0 / pivot)
                for k in range(j + 1, size):
                    cols[k] = cols[k] - ratio * cols[k][j : j + 1, :]
                left = left - ratio * left[j : j + 1, :]
                right = right - ratio * right[j : j + 1, :]
        left = jnp.where(lane >= first, left * scale, 0.0)
        right = right * scale
        work[first : first + size, 0:R] = left
        work[first : first + size, R : 2 * R] = right
        below = first + size
        if below < R:
            ph, pm, pw = split3(jnp.concatenate([left, right], 1))
            wh, wm, ww = split3(jnp.where(lane >= below, left, 0.0))
            a = jnp.concatenate([wh, wh, wm, wm, wh, ww], 0).astype(bf16)
            b = jnp.concatenate([ph, pm, ph, pm, pw, ph], 0).astype(bf16)
            update = lax.dot_general(a, b, (((0,), (0,)), ((), ())), preferred_element_type=f32)
            work[below:R, :] = work[below:R, :] - update[below:R, :]


def iterate_kernel(
    m_hbm, q_hbm, lr_ref, rr_ref, d_ref,
    m, f, ms, ring, ls, ly, lz, la, gc, gx, gs, work, rcs, rc, rzs, rz, rx, ra, cy, cz, cc, scale,
    m_sem, q_sem, ring_s, ring_r, ly_s, ly_r, lz_s, lz_r, la_s, la_r, gc_s, gc_r, gx_s, gx_r,
    rc_s, rc_r, rz_s, rz_r, rx_s, rx_r, ra_s, ra_r, rm_s, rm_r, cy_s, cy_r, cz_s, cz_r, cc_s, cc_r,
):
    z, fs, y = lax.axis_index("replica"), lax.axis_index("fsdp"), lax.axis_index("tensor")
    x, c = fs // 2, lax.rem(fs, 2)
    mate = {"fsdp": x * 2 + 1 - c}

    def at_y(k):
        return {"tensor": lax.rem(y + k, NY)}

    def at_z(k):
        return {"replica": lax.rem(z + k, NZ)}

    def at_x(k):
        return {"fsdp": lax.rem(x + k, NX) * 2 + c}

    def copy(src, dst, send, recv, to):
        return pltpu.make_async_remote_copy(
            src_ref=src, dst_ref=dst, send_sem=send, recv_sem=recv, device_id=to, device_id_type=MESH
        )

    load_m = pltpu.make_async_copy(m_hbm, m, m_sem)
    load_m.start()
    load_q = pltpu.make_async_copy(q_hbm, f, q_sem)
    load_q.start()
    barrier = pltpu.get_barrier_semaphore()
    for k in range(1, NY):
        pl.semaphore_signal(barrier, inc=1, device_id=at_y(k), device_id_type=MESH)
    for k in range(1, NZ):
        pl.semaphore_signal(barrier, inc=1, device_id=at_z(k), device_id_type=MESH)
    for k in range(1, NX):
        pl.semaphore_signal(barrier, inc=1, device_id=at_x(k), device_id_type=MESH)
    pl.semaphore_signal(barrier, inc=1, device_id=mate, device_id_type=MESH)
    scale[...] = jnp.full((8, R), 1.0 / NZ, f32)
    load_q.wait()
    load_m.wait()
    ls[...] = jnp.dot(m[...], f[...], preferred_element_type=f32).astype(bf16)
    pl.semaphore_wait(barrier, NY + NZ + NX - 2)

    def chunk(way, j):
        return pl.ds(pl.multiple_of(lax.rem(j + 2 * NZ, NZ) * LZ + way * HZ, HZ), HZ)

    def ring_copy(way, step):
        step_to = 1 if way == 0 else NZ - 1
        if step == 1:
            src = m.at[chunk(way, z - 1 if way == 0 else z + 1)]
        else:
            src = ring.at[way, step - 2]
        return copy(src, ring.at[way, step - 1], ring_s.at[way, step - 1],
                    ring_r.at[way, step - 1], at_z(step_to))

    def ring_step(step):
        for way in range(2):
            if step > 1:
                ring_copy(way, step - 1).wait_recv()
                own = m[chunk(way, z - step if way == 0 else z + step), :].astype(f32)
                ring[way, step - 2] = (ring[way, step - 2].astype(f32) + own).astype(bf16)
            ring_copy(way, step).start()

    def ring_end():
        for way in range(2):
            ring_copy(way, NZ - 1).wait_recv()
            total = ring[way, NZ - 2].astype(f32) + m[chunk(way, z), :].astype(f32)
            high = total.astype(bf16)
            ms[way * HZ : (way + 1) * HZ, :] = high
            ms[LZ + way * HZ : LZ + (way + 1) * HZ, :] = (total - high.astype(f32)).astype(bf16)

    def sums_over_z(it):
        for k in range(1, NZ):
            s = lax.rem(z + k, NZ)
            copy(cz.at[it, s], cz.at[it, s], cz_s.at[k], cz_r.at[it, s], at_z(k)).wait_recv()
        total = cz[it, 0]
        for s in range(1, NZ):
            total = total + cz[it, s]
        cc[it, 0] = total
        copy(cc.at[it, 0], cc.at[it, 1], cc_s, cc_r.at[it], mate).start()

    def column_scale(it):
        copy(cc.at[it, 0], cc.at[it, 1], cc_s, cc_r.at[it], mate).wait()
        scale[...] = math.sqrt(FF) / jnp.sqrt(cc[it, 0] + cc[it, 1] + norm_eps)

    def left_first(it, start):
        for k in range(1, NY):
            t = lax.rem(y + k, NY)
            start(copy(ls.at[pl.ds(t * LY, LY)], ly.at[it, y], ly_s.at[k], ly_r.at[it, y], at_y(k)))
        ring_step(1)
        total = ls[pl.ds(y * LY, LY), :].astype(f32)
        for k in range(1, NY):
            s = lax.rem(y + k, NY)
            copy(ly.at[it, s], ly.at[it, s], ly_s.at[k], ly_r.at[it, s], at_y(k)).wait_recv()
            total = total + ly[it, s].astype(f32)
        lz[z] = total.astype(bf16)
        for k in range(1, NZ):
            start(copy(lz.at[z], lz.at[z], lz_s.at[k], lz_r.at[z], at_z(k)))
        ring_step(2)
        for k in range(1, NZ):
            s = lax.rem(z + k, NZ)
            copy(lz.at[s], lz.at[s], lz_s.at[k], lz_r.at[s], at_z(k)).wait_recv()
        total = lz[0].astype(f32)
        for s in range(1, NZ):
            total = total + lz[s].astype(f32)
        la[it, pl.ds(y * LY, LY), :] = (total * scale[0:1, :]).astype(bf16)
        mine = la.at[it, pl.ds(y * LY, LY)]
        for k in range(1, NY):
            start(copy(mine, mine, la_s.at[k], la_r.at[it, y], at_y(k)))
        ring_step(3)
        for k in range(1, NY):
            s = lax.rem(y + k, NY)
            theirs = la.at[it, pl.ds(s * LY, LY)]
            copy(theirs, theirs, la_s.at[k], la_r.at[it, s], at_y(k)).wait_recv()

    def left_later(it, start):
        both = jnp.dot(ms[...], f[...], preferred_element_type=f32)
        ly[it, y] = (both[0:LZ, :] + both[LZ : 2 * LZ, :]).astype(bf16)
        for k in range(1, NY):
            start(copy(ly.at[it, y], ly.at[it, y], ly_s.at[k], ly_r.at[it, y], at_y(k)))
        sums_over_z(it - 1)
        for k in range(1, NY):
            s = lax.rem(y + k, NY)
            copy(ly.at[it, s], ly.at[it, s], ly_s.at[k], ly_r.at[it, s], at_y(k)).wait_recv()
        column_scale(it - 1)
        total = ly[it, 0].astype(f32)
        for s in range(1, NY):
            total = total + ly[it, s].astype(f32)
        rows = (total * (scale[0:1, :] * (1.0 / NZ))).astype(bf16)
        la[it, pl.ds(z * LZ, LZ), :] = rows
        mine = la.at[it, pl.ds(z * LZ, LZ)]
        for k in range(1, NZ):
            start(copy(mine, mine, la_s.at[k], la_r.at[it, z], at_z(k)))
        return rows

    def wait_left_later(it):
        for k in range(1, NZ):
            s = lax.rem(z + k, NZ)
            theirs = la.at[it, pl.ds(s * LZ, LZ)]
            copy(theirs, theirs, la_s.at[k], la_r.at[it, s], at_z(k)).wait_recv()

    def product(block, left, half):
        columns = pl.ds(pl.multiple_of(half * RC, 128), RC)
        return lax.dot_general(
            block[:, columns], left, (((0,), (0,)), ((), ())), preferred_element_type=f32
        ).reshape(NZ, RZ, R)

    def iteration(it, first):
        sends = []

        def start(cp):
            cp.start()
            sends.append(cp)

        def gram_to_mate():
            left = la[it]
            gs[...] = lax.dot_general(
                left, left, (((0,), (0,)), ((), ())), preferred_element_type=f32
            )
            start(copy(gs, gc.at[it], gc_s, gc_r.at[it], mate))

        def gram_over_x():
            copy(gs, gc.at[it], gc_s, gc_r.at[it], mate).wait_recv()
            gx[it, x] = (gs[...] + gc[it]).astype(bf16)
            for k in range(1, NX):
                start(copy(gx.at[it, x], gx.at[it, x], gx_s.at[k], gx_r.at[it, x], at_x(k)))

        if first:
            left_first(it, start)
            ring_step(4)
            gram_to_mate()
            block, rows = m, la[it]
        else:
            rows = left_later(it, start)
            block, rows = ms, jnp.concatenate([rows, rows], 0)

        rcs[...] = product(block, rows, 1 - c)
        to_mate = []
        for p, (row, size) in enumerate(PARTS):
            part = pl.ds(row, size)
            cp = copy(rcs.at[:, part], rc.at[it, :, part], rc_s.at[p], rc_r.at[it, p], mate)
            start(cp)
            to_mate.append(cp)
        own = product(block, rows, c)
        if first:
            gram_over_x()
        for p, (row, size) in enumerate(PARTS):
            part = pl.ds(row, size)
            to_mate[p].wait_recv()
            rzs[:, part] = (own[:, row : row + size] + rc[it, :, part]).astype(bf16)
            for k in range(1, NZ):
                t = lax.rem(z + k, NZ)
                start(copy(rzs.at[t, part], rz.at[it, z, part],
                           rz_s.at[p, k], rz_r.at[it, p, z], at_z(k)))
        if first:
            ring_step(5)
        else:
            wait_left_later(it)
            gram_to_mate()
            gram_over_x()

        for p, (row, size) in enumerate(PARTS):
            part = pl.ds(row, size)
            total = rzs[z, part].astype(f32)
            for k in range(1, NZ):
                s = lax.rem(z + k, NZ)
                there = rz.at[it, s, part]
                copy(there, there, rz_s.at[p, k], rz_r.at[it, p, s], at_z(k)).wait_recv()
                total = total + rz[it, s, part].astype(f32)
            rx[it, x, part] = total.astype(bf16)
            here = rx.at[it, x, part]
            for k in range(1, NX):
                start(copy(here, here, rx_s.at[p, k], rx_r.at[it, p, x], at_x(k)))
        if first:
            ring_step(6)

        for k in range(1, NX):
            s = lax.rem(x + k, NX)
            copy(gx.at[it, s], gx.at[it, s], gx_s.at[k], gx_r.at[it, s], at_x(k)).wait_recv()
        gram = (gx[it, 0].astype(f32) + gx[it, 1].astype(f32)) + (
            gx[it, 2].astype(f32) + gx[it, 3].astype(f32)
        )
        eye = lax.broadcasted_iota(jnp.int32, (R, R), 0) == lax.broadcasted_iota(
            jnp.int32, (R, R), 1
        )
        ridge = (ridge_scale / R) * jnp.sum(jnp.where(eye, gram, 0.0), keepdims=True)
        work[:, 0:R] = jnp.where(eye, gram + ridge, gram)
        work[:, R : 2 * R] = jnp.where(eye, 1.0, 0.0)
        factor_inverse(work)

        squares = jnp.zeros((1, R), f32)
        for p, (row, size) in enumerate(PARTS):
            part = pl.ds(row, size)
            for k in range(1, NX):
                s = lax.rem(x + k, NX)
                there = rx.at[it, s, part]
                copy(there, there, rx_s.at[p, k], rx_r.at[it, p, s], at_x(k)).wait_recv()
            total = (rx[it, 0, part].astype(f32) + rx[it, 1, part].astype(f32)) + (
                rx[it, 2, part].astype(f32) + rx[it, 3, part].astype(f32)
            )
            right = lax.dot_general(
                total, work[:, R : 2 * R], (((1,), (1,)), ((), ())),
                preferred_element_type=f32, precision=HIGHEST,
            ) * (1.0 / NZ)
            ra[it, c, z, part] = right.astype(bf16)
            mine = ra.at[it, c, z, part]
            for k in range(1, NZ):
                start(copy(mine, mine, ra_s.at[p, k], ra_r.at[it, p, z], at_z(k)))
            squares = squares + jnp.sum(right * right, axis=0, keepdims=True)
        cy[it, y] = jnp.broadcast_to(squares, (8, R))
        for k in range(1, NY):
            start(copy(cy.at[it, y], cy.at[it, y], cy_s.at[k], cy_r.at[it, y], at_y(k)))
        if first:
            ring_step(7)
        for k in range(1, NY):
            s = lax.rem(y + k, NY)
            copy(cy.at[it, s], cy.at[it, s], cy_s.at[k], cy_r.at[it, s], at_y(k)).wait_recv()
        total = cy[it, 0]
        for s in range(1, NY):
            total = total + cy[it, s]
        cz[it, z] = total
        for k in range(1, NZ):
            start(copy(cz.at[it, z], cz.at[it, z], cz_s.at[k], cz_r.at[it, z], at_z(k)))
        for p, (row, size) in enumerate(PARTS):
            part = pl.ds(row, size)
            for k in range(1, NZ):
                s = lax.rem(z + k, NZ)
                there = ra.at[it, c, s, part]
                copy(there, there, ra_s.at[p, k], ra_r.at[it, p, s], at_z(k)).wait_recv()
            half = ra.at[it, c, :, part]
            start(copy(half, half, rm_s.at[p], rm_r.at[it, p], mate))
        if first:
            ring_end()
        for p, (row, size) in enumerate(PARTS):
            half = ra.at[it, 1 - c, :, pl.ds(row, size)]
            copy(half, half, rm_s.at[p], rm_r.at[it, p], mate).wait_recv()
        f[...] = ra[it].reshape(COLS, R)
        for cp in sends:
            cp.wait_send()
        if first:
            for way in range(2):
                for step in range(1, NZ):
                    ring_copy(way, step).wait_send()

    iteration(0, True)

    def again(it, carry):
        iteration(it, False)
        return carry

    lax.fori_loop(1, ITERS, again, 0)
    last = ITERS - 1
    lr_ref[...] = lax.dot_general(
        la[last].astype(f32), work[:, R : 2 * R], (((1,), (1,)), ((), ())),
        preferred_element_type=f32, precision=HIGHEST,
    ).astype(bf16)
    rr_ref[...] = f[...]
    sums_over_z(last)
    column_scale(last)
    d_ref[...] = scale[...]


def iterate(block, q):
    vmem = pl.BlockSpec(memory_space=pltpu.VMEM)
    hbm = pl.BlockSpec(memory_space=pltpu.HBM)
    dma = pltpu.SemaphoreType.DMA
    n, parts = ITERS, len(PARTS)
    return pl.pallas_call(
        iterate_kernel,
        out_shape=[
            jax.ShapeDtypeStruct((ROWS, R), bf16),
            jax.ShapeDtypeStruct((COLS, R), bf16),
            jax.ShapeDtypeStruct((8, R), f32),
        ],
        in_specs=[hbm, hbm],
        out_specs=[vmem] * 3,
        scratch_shapes=[
            pltpu.VMEM((ROWS, COLS), bf16),
            pltpu.VMEM((COLS, R), bf16),
            pltpu.VMEM((2 * LZ, COLS), bf16),
            pltpu.VMEM((2, NZ - 1, HZ, COLS), bf16),
            pltpu.VMEM((ROWS, R), bf16),
            pltpu.VMEM((n, NY, LY, R), bf16),
            pltpu.VMEM((NZ, LY, R), bf16),
            pltpu.VMEM((n, ROWS, R), bf16),
            pltpu.VMEM((n, R, R), f32),
            pltpu.VMEM((n, NX, R, R), bf16),
            pltpu.VMEM((R, R), f32),
            pltpu.VMEM((R, 2 * R), f32),
            pltpu.VMEM((NZ, RZ, R), f32),
            pltpu.VMEM((n, NZ, RZ, R), f32),
            pltpu.VMEM((NZ, RZ, R), bf16),
            pltpu.VMEM((n, NZ, RZ, R), bf16),
            pltpu.VMEM((n, NX, RZ, R), bf16),
            pltpu.VMEM((n, 2, NZ, RZ, R), bf16),
            pltpu.VMEM((n, NY, 8, R), f32),
            pltpu.VMEM((n, NZ, 8, R), f32),
            pltpu.VMEM((n, 2, 8, R), f32),
            pltpu.VMEM((8, R), f32),
            dma(()), dma(()),
            dma((2, NZ - 1)), dma((2, NZ - 1)),
            dma((NY,)), dma((n, NY)),
            dma((NZ,)), dma((NZ,)),
            dma((NY,)), dma((n, NY)),
            dma(()), dma((n,)),
            dma((NX,)), dma((n, NX)),
            dma((parts,)), dma((n, parts)),
            dma((parts, NZ)), dma((n, parts, NZ)),
            dma((parts, NX)), dma((n, parts, NX)),
            dma((parts, NZ)), dma((n, parts, NZ)),
            dma((parts,)), dma((n, parts)),
            dma((NY,)), dma((n, NY)),
            dma((NZ,)), dma((n, NZ)),
            dma(()), dma((n,)),
        ],
        compiler_params=pltpu.CompilerParams(
            collective_id=0, has_side_effects=True, vmem_limit_bytes=56 << 20
        ),
        cost_estimate=pl.CostEstimate(
            flops=12 * ROWS * COLS * R, bytes_accessed=2 * ROWS * COLS, transcendentals=0
        ),
    )(block, q)


def finish_kernel(m, left, right, scale, m_out, u_out, q_out):
    correction = lax.dot_general(
        left[...], right[...], (((1,), (1,)), ((), ())), preferred_element_type=f32
    )
    m_out[...] = (m[...].astype(f32) - (1.0 - momentum_decay) * correction).astype(bf16)
    u_out[...] = math.sqrt(D) * left[...].astype(f32)

    @pl.when(pl.program_id(0) == 0)
    def _():
        q_out[...] = (right[...].astype(f32) * scale[0:1, :]).astype(bf16)


def finish(block, left, right, scale):
    steps = 2
    rows = ROWS // steps
    return pl.pallas_call(
        finish_kernel,
        grid=(steps,),
        out_shape=[
            jax.ShapeDtypeStruct((ROWS, COLS), bf16),
            jax.ShapeDtypeStruct((ROWS, R), f32),
            jax.ShapeDtypeStruct((COLS, R), bf16),
        ],
        in_specs=[
            pl.BlockSpec((rows, COLS), lambda i: (i, 0)),
            pl.BlockSpec((rows, R), lambda i: (i, 0)),
            pl.BlockSpec((COLS, R), lambda i: (0, 0)),
            pl.BlockSpec((8, R), lambda i: (0, 0)),
        ],
        out_specs=[
            pl.BlockSpec((rows, COLS), lambda i: (i, 0)),
            pl.BlockSpec((rows, R), lambda i: (i, 0)),
            pl.BlockSpec((COLS, R), lambda i: (0, 0)),
        ],
        compiler_params=pltpu.CompilerParams(vmem_limit_bytes=56 << 20),
        cost_estimate=pl.CostEstimate(
            flops=2 * ROWS * COLS * R, bytes_accessed=4 * ROWS * COLS, transcendentals=0
        ),
    )(block, left, right, scale)


def shards(momentum, q_prev):
    block = momentum[0]
    left, right, scale = iterate(block, q_prev)
    momentum_next, update_left, q_next = finish(block, left, right, scale)
    return momentum_next[None], update_left, q_next


def solution(mesh):
    in_specs = (P("replica", "fsdp", "tensor"), P("tensor", None))
    out_specs = (P("replica", "fsdp", "tensor"), P("fsdp", None), P("tensor", None))
    return jax.shard_map(shards, mesh=mesh, in_specs=in_specs, out_specs=out_specs, check_vma=False)
```

```python
import functools
import math

import jax
import jax.numpy as jnp
from jax import lax
from jax.experimental import pallas as pl
from jax.experimental.pallas import tpu as pltpu
from jax.sharding import PartitionSpec as P

D = 4096
FF = 14336
R = 128
ITERS = 3
NY, NZ, NX = 8, 8, 4
ROWS = 512
COLS = 1792
LY = ROWS // NY
LZ = ROWS // NZ
HZ = LZ // 2
RC = COLS // 2
RZ = RC // NZ
RING = (4, 3, 5, 2, 6, 1, 7)
RING_X = (2, 1, 3)

ridge_scale = 1e-06
norm_eps = 1e-06
momentum_decay = 0.95

MESH = pl.DeviceIdType.MESH
f32, bf16 = jnp.float32, jnp.bfloat16
HIGHEST = lax.Precision.HIGHEST


def split3(w):
    high = w.astype(bf16).astype(f32)
    rest = w - high
    mid = rest.astype(bf16).astype(f32)
    return high, mid, rest - mid


def factor_inverse(work):
    size = 16
    sub = lax.broadcasted_iota(jnp.int32, (size, R), 0)
    lane = lax.broadcasted_iota(jnp.int32, (size, R), 1)
    for first in range(0, R, size):
        left, right = work[first : first + size, 0:R], work[first : first + size, R : 2 * R]
        cols = [
            jnp.broadcast_to(left[:, first + k : first + k + 1], (size, R)) for k in range(size)
        ]
        scale = jnp.zeros((size, R), f32)
        for j in range(size):
            pivot = jnp.broadcast_to(cols[j][j : j + 1, :], (size, R))
            scale = jnp.where(sub == j, lax.rsqrt(pivot), scale)
            if j < size - 1:
                ratio = jnp.where(sub > j, cols[j], 0.0) * (1.0 / pivot)
                for k in range(j + 1, size):
                    cols[k] = cols[k] - ratio * cols[k][j : j + 1, :]
                left = left - ratio * left[j : j + 1, :]
                right = right - ratio * right[j : j + 1, :]
        left = jnp.where(lane >= first, left * scale, 0.0)
        right = right * scale
        work[first : first + size, 0:R] = left
        work[first : first + size, R : 2 * R] = right
        below = first + size
        if below < R:
            ph, pm, pw = split3(jnp.concatenate([left, right], 1))
            wh, wm, ww = split3(jnp.where(lane >= below, left, 0.0))
            a = jnp.concatenate([wh, wh, wm, wm, wh, ww], 0).astype(bf16)
            b = jnp.concatenate([ph, pm, ph, pm, pw, ph], 0).astype(bf16)
            update = lax.dot_general(a, b, (((0,), (0,)), ((), ())), preferred_element_type=f32)
            work[below:R, :] = work[below:R, :] - update[below:R, :]


def iterate_kernel(
    m_hbm, q_hbm, lr_ref, rr_ref, d_ref,
    m, ms, ring, ls, ly, lz, la, gc, gx, gs, work, rcs, rc, rzs, rz, rx, ra, cy, cz, cc, scale,
    m_sem, q_sem, ring_s, ring_r, ly_s, ly_r, lz_s, lz_r, la_s, la_r, gc_s, gc_r, gx_s, gx_r,
    rc_s, rc_r, rz_s, rz_r, rx_s, rx_r, ra_s, ra_r, rm_s, rm_r, cy_s, cy_r, cz_s, cz_r, cc_s, cc_r,
):
    z, fs, y = lax.axis_index("replica"), lax.axis_index("fsdp"), lax.axis_index("tensor")
    x, c = fs // 2, lax.rem(fs, 2)
    mate = {"fsdp": x * 2 + 1 - c}

    def at_y(k):
        return {"tensor": lax.rem(y + k, NY)}

    def at_z(k):
        return {"replica": lax.rem(z + k, NZ)}

    def at_x(k):
        return {"fsdp": lax.rem(x + k, NX) * 2 + c}

    def copy(src, dst, send, recv, to):
        return pltpu.make_async_remote_copy(
            src_ref=src, dst_ref=dst, send_sem=send, recv_sem=recv, device_id=to, device_id_type=MESH
        )

    def factor(it):
        return ra[it].reshape(COLS, R)

    load_m = pltpu.make_async_copy(m_hbm, m, m_sem)
    load_m.start()
    load_q = pltpu.make_async_copy(q_hbm, ra.at[0], q_sem)
    load_q.start()
    barrier = pltpu.get_barrier_semaphore()
    for k in range(1, NY):
        pl.semaphore_signal(barrier, inc=1, device_id=at_y(k), device_id_type=MESH)
    for k in range(1, NZ):
        pl.semaphore_signal(barrier, inc=1, device_id=at_z(k), device_id_type=MESH)
    for k in range(1, NX):
        pl.semaphore_signal(barrier, inc=1, device_id=at_x(k), device_id_type=MESH)
    pl.semaphore_signal(barrier, inc=1, device_id=mate, device_id_type=MESH)
    scale[...] = jnp.full((8, R), 1.0 / NZ, f32)
    load_q.wait()
    load_m.wait()
    ls[...] = jnp.dot(m[...], factor(0), preferred_element_type=f32).astype(bf16)
    pl.semaphore_wait(barrier, NY + NZ + NX - 2)

    def chunk(way, j):
        return pl.ds(pl.multiple_of(lax.rem(j + 2 * NZ, NZ) * LZ + way * HZ, HZ), HZ)

    def ring_copy(way, step):
        step_to = 1 if way == 0 else NZ - 1
        if step == 1:
            src = m.at[chunk(way, z - 1 if way == 0 else z + 1)]
        else:
            src = ring.at[way, step - 2]
        return copy(src, ring.at[way, step - 1], ring_s.at[way, step - 1],
                    ring_r.at[way, step - 1], at_z(step_to))

    def ring_step(step):
        for way in range(2):
            if step > 1:
                ring_copy(way, step - 1).wait_recv()
                own = m[chunk(way, z - step if way == 0 else z + step), :].astype(f32)
                ring[way, step - 2] = (ring[way, step - 2].astype(f32) + own).astype(bf16)
            ring_copy(way, step).start()

    def ring_end():
        for way in range(2):
            ring_copy(way, NZ - 1).wait_recv()
            total = ring[way, NZ - 2].astype(f32) + m[chunk(way, z), :].astype(f32)
            high = total.astype(bf16)
            ms[way * HZ : (way + 1) * HZ, :] = high
            ms[LZ + way * HZ : LZ + (way + 1) * HZ, :] = (total - high.astype(f32)).astype(bf16)

    def triangular(rows):
        return lax.dot_general(
            rows, work[:, R : 2 * R], (((1,), (1,)), ((), ())),
            preferred_element_type=f32, precision=HIGHEST,
        )

    def sums_over_z(it):
        for k in RING:
            s = lax.rem(z + k, NZ)
            copy(cz.at[it, s], cz.at[it, s], cz_s.at[k], cz_r.at[it, s], at_z(k)).wait_recv()
        total = cz[it, 0]
        for s in range(1, NZ):
            total = total + cz[it, s]
        cc[it, 0] = total
        copy(cc.at[it, 0], cc.at[it, 1], cc_s, cc_r.at[it], mate).start()

    def column_scale(it):
        copy(cc.at[it, 0], cc.at[it, 1], cc_s, cc_r.at[it], mate).wait()
        scale[...] = math.sqrt(FF) / jnp.sqrt(cc[it, 0] + cc[it, 1] + norm_eps)

    def left_first(it, start):
        for k in RING:
            t = lax.rem(y + k, NY)
            start(copy(ls.at[pl.ds(t * LY, LY)], ly.at[it, y], ly_s.at[k], ly_r.at[it, y], at_y(k)))
        ring_step(1)
        total = ls[pl.ds(y * LY, LY), :].astype(f32)
        for k in RING:
            s = lax.rem(y + k, NY)
            copy(ly.at[it, s], ly.at[it, s], ly_s.at[k], ly_r.at[it, s], at_y(k)).wait_recv()
            total = total + ly[it, s].astype(f32)
        lz[z] = total.astype(bf16)
        for k in RING:
            start(copy(lz.at[z], lz.at[z], lz_s.at[k], lz_r.at[z], at_z(k)))
        ring_step(2)
        for k in RING:
            s = lax.rem(z + k, NZ)
            copy(lz.at[s], lz.at[s], lz_s.at[k], lz_r.at[s], at_z(k)).wait_recv()
        total = lz[0].astype(f32)
        for s in range(1, NZ):
            total = total + lz[s].astype(f32)
        la[it, pl.ds(y * LY, LY), :] = (total * scale[0:1, :]).astype(bf16)
        mine = la.at[it, pl.ds(y * LY, LY)]
        for k in RING:
            start(copy(mine, mine, la_s.at[k], la_r.at[it, y], at_y(k)))
        ring_step(3)
        for k in RING:
            s = lax.rem(y + k, NY)
            theirs = la.at[it, pl.ds(s * LY, LY)]
            copy(theirs, theirs, la_s.at[k], la_r.at[it, s], at_y(k)).wait_recv()

    def left_later(it, start):
        both = jnp.dot(ms[...], factor(it), preferred_element_type=f32)
        ly[it, y] = (both[0:LZ, :] + both[LZ : 2 * LZ, :]).astype(bf16)
        for k in RING:
            start(copy(ly.at[it, y], ly.at[it, y], ly_s.at[k], ly_r.at[it, y], at_y(k)))
        sums_over_z(it - 1)
        for k in RING:
            s = lax.rem(y + k, NY)
            copy(ly.at[it, s], ly.at[it, s], ly_s.at[k], ly_r.at[it, s], at_y(k)).wait_recv()
        column_scale(it - 1)
        total = ly[it, 0].astype(f32)
        for s in range(1, NY):
            total = total + ly[it, s].astype(f32)
        rows = (triangular(total) * (scale[0:1, :] * (1.0 / NZ**2))).astype(bf16)
        la[it, pl.ds(z * LZ, LZ), :] = rows
        mine = la.at[it, pl.ds(z * LZ, LZ)]
        for k in RING:
            start(copy(mine, mine, la_s.at[k], la_r.at[it, z], at_z(k)))
        return rows

    def wait_left_later(it):
        for k in RING:
            s = lax.rem(z + k, NZ)
            theirs = la.at[it, pl.ds(s * LZ, LZ)]
            copy(theirs, theirs, la_s.at[k], la_r.at[it, s], at_z(k)).wait_recv()

    def product(block, left, half):
        columns = pl.ds(pl.multiple_of(half * RC, 128), RC)
        return lax.dot_general(
            block[:, columns], left, (((0,), (0,)), ((), ())), preferred_element_type=f32
        ).reshape(NZ, RZ, R)

    def iteration(it):
        first, final = it == 0, it == ITERS - 1
        sends = []

        def start(cp):
            cp.start()
            sends.append(cp)

        def gram_to_mate():
            left = la[it]
            gs[...] = lax.dot_general(
                left, left, (((0,), (0,)), ((), ())), preferred_element_type=f32
            )
            start(copy(gs, gc.at[it], gc_s, gc_r.at[it], mate))

        def gram_over_x():
            copy(gs, gc.at[it], gc_s, gc_r.at[it], mate).wait_recv()
            gx[it, x] = (gs[...] + gc[it]).astype(bf16)
            for k in RING_X:
                start(copy(gx.at[it, x], gx.at[it, x], gx_s.at[k], gx_r.at[it, x], at_x(k)))

        def factorise():
            for k in RING_X:
                s = lax.rem(x + k, NX)
                copy(gx.at[it, s], gx.at[it, s], gx_s.at[k], gx_r.at[it, s], at_x(k)).wait_recv()
            gram = (gx[it, 0].astype(f32) + gx[it, 1].astype(f32)) + (
                gx[it, 2].astype(f32) + gx[it, 3].astype(f32)
            )
            eye = lax.broadcasted_iota(jnp.int32, (R, R), 0) == lax.broadcasted_iota(
                jnp.int32, (R, R), 1
            )
            ridge = (ridge_scale / R) * jnp.sum(jnp.where(eye, gram, 0.0), keepdims=True)
            work[:, 0:R] = jnp.where(eye, gram + ridge, gram)
            work[:, R : 2 * R] = jnp.where(eye, 1.0, 0.0)
            factor_inverse(work)

        def gather(rows):
            ra[it + 1, c, z] = rows.astype(bf16)
            mine = ra.at[it + 1, c, z]
            for k in RING:
                start(copy(mine, mine, ra_s.at[k], ra_r.at[it, z], at_z(k)))

        def squares(right):
            cy[it, y] = jnp.broadcast_to(jnp.sum(right * right, axis=0, keepdims=True), (8, R))
            for k in RING:
                start(copy(cy.at[it, y], cy.at[it, y], cy_s.at[k], cy_r.at[it, y], at_y(k)))

        def squares_over_y():
            for k in RING:
                s = lax.rem(y + k, NY)
                copy(cy.at[it, s], cy.at[it, s], cy_s.at[k], cy_r.at[it, s], at_y(k)).wait_recv()
            total = cy[it, 0]
            for s in range(1, NY):
                total = total + cy[it, s]
            cz[it, z] = total
            for k in RING:
                start(copy(cz.at[it, z], cz.at[it, z], cz_s.at[k], cz_r.at[it, z], at_z(k)))

        if first:
            left_first(it, start)
            ring_step(4)
            gram_to_mate()
            block, rows = m, la[it]
        else:
            rows = left_later(it, start)
            block, rows = ms, jnp.concatenate([rows, rows], 0)

        rcs[...] = product(block, rows, 1 - c).astype(bf16)
        to_mate = copy(rcs, rc.at[it], rc_s, rc_r.at[it], mate)
        start(to_mate)
        own = product(block, rows, c)
        if first:
            gram_over_x()
        to_mate.wait_recv()
        rzs[...] = (own + rc[it].astype(f32)).astype(bf16)
        for k in RING:
            t = lax.rem(z + k, NZ)
            start(copy(rzs.at[t], rz.at[it, z], rz_s.at[k], rz_r.at[it, z], at_z(k)))
        if first:
            ring_step(5)
        else:
            wait_left_later(it)
            gram_to_mate()
            gram_over_x()

        total = rzs[z].astype(f32)
        for k in RING:
            s = lax.rem(z + k, NZ)
            copy(rz.at[it, s], rz.at[it, s], rz_s.at[k], rz_r.at[it, s], at_z(k)).wait_recv()
            total = total + rz[it, s].astype(f32)
        rx[it, x] = total.astype(bf16)
        for k in RING_X:
            start(copy(rx.at[it, x], rx.at[it, x], rx_s.at[k], rx_r.at[it, x], at_x(k)))
        if first:
            ring_step(6)
        if final:
            factorise()
        for k in RING_X:
            s = lax.rem(x + k, NX)
            copy(rx.at[it, s], rx.at[it, s], rx_s.at[k], rx_r.at[it, s], at_x(k)).wait_recv()
        total = (rx[it, 0].astype(f32) + rx[it, 1].astype(f32)) + (
            rx[it, 2].astype(f32) + rx[it, 3].astype(f32)
        )

        if final:
            right = triangular(total) * (1.0 / NZ)
            gather(right)
            squares(right)
            squares_over_y()
        else:
            gather(total)
            if first:
                ring_step(7)
            factorise()
            squares(triangular(total) * (1.0 / NZ))
        for k in RING:
            s = lax.rem(z + k, NZ)
            there = ra.at[it + 1, c, s]
            copy(there, there, ra_s.at[k], ra_r.at[it, s], at_z(k)).wait_recv()
        half = ra.at[it + 1, c]
        start(copy(half, half, rm_s, rm_r.at[it], mate))
        if not final:
            squares_over_y()
        if first:
            ring_end()
        half = ra.at[it + 1, 1 - c]
        copy(half, half, rm_s, rm_r.at[it], mate).wait_recv()
        for cp in sends:
            cp.wait_send()
        if first:
            for way in range(2):
                for step in range(1, NZ):
                    ring_copy(way, step).wait_send()

    for it in range(ITERS):
        iteration(it)
    last = ITERS - 1
    lr_ref[...] = triangular(la[last].astype(f32)).astype(bf16)
    rr_ref[...] = factor(ITERS)
    sums_over_z(last)
    column_scale(last)
    d_ref[...] = scale[...]


def iterate(block, q):
    vmem = pl.BlockSpec(memory_space=pltpu.VMEM)
    hbm = pl.BlockSpec(memory_space=pltpu.HBM)
    dma = pltpu.SemaphoreType.DMA
    n = ITERS
    return pl.pallas_call(
        iterate_kernel,
        out_shape=[
            jax.ShapeDtypeStruct((ROWS, R), bf16),
            jax.ShapeDtypeStruct((COLS, R), bf16),
            jax.ShapeDtypeStruct((8, R), f32),
        ],
        in_specs=[hbm, hbm],
        out_specs=[vmem] * 3,
        scratch_shapes=[
            pltpu.VMEM((ROWS, COLS), bf16),
            pltpu.VMEM((2 * LZ, COLS), bf16),
            pltpu.VMEM((2, NZ - 1, HZ, COLS), bf16),
            pltpu.VMEM((ROWS, R), bf16),
            pltpu.VMEM((n, NY, LY, R), bf16),
            pltpu.VMEM((NZ, LY, R), bf16),
            pltpu.VMEM((n, ROWS, R), bf16),
            pltpu.VMEM((n, R, R), f32),
            pltpu.VMEM((n, NX, R, R), bf16),
            pltpu.VMEM((R, R), f32),
            pltpu.VMEM((R, 2 * R), f32),
            pltpu.VMEM((NZ, RZ, R), bf16),
            pltpu.VMEM((n, NZ, RZ, R), bf16),
            pltpu.VMEM((NZ, RZ, R), bf16),
            pltpu.VMEM((n, NZ, RZ, R), bf16),
            pltpu.VMEM((n, NX, RZ, R), bf16),
            pltpu.VMEM((n + 1, 2, NZ, RZ, R), bf16),
            pltpu.VMEM((n, NY, 8, R), f32),
            pltpu.VMEM((n, NZ, 8, R), f32),
            pltpu.VMEM((n, 2, 8, R), f32),
            pltpu.VMEM((8, R), f32),
            dma(()), dma(()),
            dma((2, NZ - 1)), dma((2, NZ - 1)),
            dma((NY,)), dma((n, NY)),
            dma((NZ,)), dma((NZ,)),
            dma((NY,)), dma((n, NY)),
            dma(()), dma((n,)),
            dma((NX,)), dma((n, NX)),
            dma(()), dma((n,)),
            dma((NZ,)), dma((n, NZ)),
            dma((NX,)), dma((n, NX)),
            dma((NZ,)), dma((n, NZ)),
            dma(()), dma((n,)),
            dma((NY,)), dma((n, NY)),
            dma((NZ,)), dma((n, NZ)),
            dma(()), dma((n,)),
        ],
        compiler_params=pltpu.CompilerParams(
            collective_id=0, has_side_effects=True, vmem_limit_bytes=56 << 20
        ),
        cost_estimate=pl.CostEstimate(
            flops=12 * ROWS * COLS * R, bytes_accessed=2 * ROWS * COLS, transcendentals=0
        ),
    )(block, q.reshape(2, NZ, RZ, R))


def finish_kernel(m, left, right, scale, m_out, u_out, q_out):
    correction = lax.dot_general(
        left[...], right[...], (((1,), (1,)), ((), ())), preferred_element_type=f32
    )
    m_out[...] = (m[...].astype(f32) - (1.0 - momentum_decay) * correction).astype(bf16)
    u_out[...] = math.sqrt(D) * left[...].astype(f32)

    @pl.when(pl.program_id(0) == 0)
    def _():
        q_out[...] = (right[...].astype(f32) * scale[0:1, :]).astype(bf16)


def finish(block, left, right, scale):
    steps = 2
    rows = ROWS // steps
    return pl.pallas_call(
        finish_kernel,
        grid=(steps,),
        out_shape=[
            jax.ShapeDtypeStruct((ROWS, COLS), bf16),
            jax.ShapeDtypeStruct((ROWS, R), f32),
            jax.ShapeDtypeStruct((COLS, R), bf16),
        ],
        in_specs=[
            pl.BlockSpec((rows, COLS), lambda i: (i, 0)),
            pl.BlockSpec((rows, R), lambda i: (i, 0)),
            pl.BlockSpec((COLS, R), lambda i: (0, 0)),
            pl.BlockSpec((8, R), lambda i: (0, 0)),
        ],
        out_specs=[
            pl.BlockSpec((rows, COLS), lambda i: (i, 0)),
            pl.BlockSpec((rows, R), lambda i: (i, 0)),
            pl.BlockSpec((COLS, R), lambda i: (0, 0)),
        ],
        compiler_params=pltpu.CompilerParams(vmem_limit_bytes=56 << 20),
        cost_estimate=pl.CostEstimate(
            flops=2 * ROWS * COLS * R, bytes_accessed=4 * ROWS * COLS, transcendentals=0
        ),
    )(block, left, right, scale)


def shards(momentum, q_prev):
    block = momentum[0]
    left, right, scale = iterate(block, q_prev)
    momentum_next, update_left, q_next = finish(block, left, right, scale)
    return momentum_next[None], update_left, q_next


def solution(mesh):
    in_specs = (P("replica", "fsdp", "tensor"), P("tensor", None))
    out_specs = (P("replica", "fsdp", "tensor"), P("fsdp", None), P("tensor", None))
    return jax.shard_map(shards, mesh=mesh, in_specs=in_specs, out_specs=out_specs, check_vma=False)
```

```python
import functools
import math

import jax
import jax.numpy as jnp
from jax import lax
from jax.experimental import pallas as pl
from jax.experimental.pallas import tpu as pltpu
from jax.sharding import PartitionSpec as P

D = 4096
FF = 14336
R = 128
ITERS = 3
NY, NZ, NX = 8, 8, 4
ROWS = 512
COLS = 1792
LY = ROWS // NY
LZ = ROWS // NZ
LINKS = (4, 3)
RC = COLS // 2
RZ = RC // NZ
RING = (4, 3, 5, 2, 6, 1, 7)
RING_X = (2, 1, 3)

ridge_scale = 1e-06
norm_eps = 1e-06
momentum_decay = 0.95

MESH = pl.DeviceIdType.MESH
f32, bf16 = jnp.float32, jnp.bfloat16
HIGHEST = lax.Precision.HIGHEST


def split3(w):
    high = w.astype(bf16).astype(f32)
    rest = w - high
    mid = rest.astype(bf16).astype(f32)
    return high, mid, rest - mid


def factor_inverse(work):
    size = 16
    sub = lax.broadcasted_iota(jnp.int32, (size, R), 0)
    lane = lax.broadcasted_iota(jnp.int32, (size, R), 1)
    for first in range(0, R, size):
        left, right = work[first : first + size, 0:R], work[first : first + size, R : 2 * R]
        cols = [
            jnp.broadcast_to(left[:, first + k : first + k + 1], (size, R)) for k in range(size)
        ]
        scale = jnp.zeros((size, R), f32)
        for j in range(size):
            pivot = jnp.broadcast_to(cols[j][j : j + 1, :], (size, R))
            scale = jnp.where(sub == j, lax.rsqrt(pivot), scale)
            if j < size - 1:
                ratio = jnp.where(sub > j, cols[j], 0.0) * (1.0 / pivot)
                for k in range(j + 1, size):
                    cols[k] = cols[k] - ratio * cols[k][j : j + 1, :]
                left = left - ratio * left[j : j + 1, :]
                right = right - ratio * right[j : j + 1, :]
        left = jnp.where(lane >= first, left * scale, 0.0)
        right = right * scale
        work[first : first + size, 0:R] = left
        work[first : first + size, R : 2 * R] = right
        below = first + size
        if below < R:
            ph, pm, pw = split3(jnp.concatenate([left, right], 1))
            wh, wm, ww = split3(jnp.where(lane >= below, left, 0.0))
            a = jnp.concatenate([wh, wh, wm, wm, wh, ww], 0).astype(bf16)
            b = jnp.concatenate([ph, pm, ph, pm, pw, ph], 0).astype(bf16)
            update = lax.dot_general(a, b, (((0,), (0,)), ((), ())), preferred_element_type=f32)
            work[below:R, :] = work[below:R, :] - update[below:R, :]


def iterate_kernel(
    m_hbm, q_hbm, lr_ref, rr_ref, d_ref,
    m, ms, ring, ls, ly, lz, la, gc, gx, gs, work, rcs, rc, rzs, rz, rx, ra, cy, cz, cc, scale,
    m_sem, q_sem, ring_s, ring_r, ly_s, ly_r, lz_s, lz_r, la_s, la_r, gc_s, gc_r, gx_s, gx_r,
    rc_s, rc_r, rz_s, rz_r, rx_s, rx_r, ra_s, ra_r, rm_s, rm_r, cy_s, cy_r, cz_s, cz_r, cc_s, cc_r,
):
    z, fs, y = lax.axis_index("replica"), lax.axis_index("fsdp"), lax.axis_index("tensor")
    x, c = fs // 2, lax.rem(fs, 2)
    mate = {"fsdp": x * 2 + 1 - c}

    def at_y(k):
        return {"tensor": lax.rem(y + k, NY)}

    def at_z(k):
        return {"replica": lax.rem(z + k, NZ)}

    def at_x(k):
        return {"fsdp": lax.rem(x + k, NX) * 2 + c}

    def copy(src, dst, send, recv, to):
        return pltpu.make_async_remote_copy(
            src_ref=src, dst_ref=dst, send_sem=send, recv_sem=recv, device_id=to, device_id_type=MESH
        )

    def factor(it):
        return ra[it].reshape(COLS, R)

    load_m = pltpu.make_async_copy(m_hbm, m, m_sem)
    load_m.start()
    load_q = pltpu.make_async_copy(q_hbm, ra.at[0], q_sem)
    load_q.start()
    barrier = pltpu.get_barrier_semaphore()
    for k in range(1, NY):
        pl.semaphore_signal(barrier, inc=1, device_id=at_y(k), device_id_type=MESH)
    for k in range(1, NZ):
        pl.semaphore_signal(barrier, inc=1, device_id=at_z(k), device_id_type=MESH)
    for k in range(1, NX):
        pl.semaphore_signal(barrier, inc=1, device_id=at_x(k), device_id_type=MESH)
    pl.semaphore_signal(barrier, inc=1, device_id=mate, device_id_type=MESH)
    scale[...] = jnp.full((8, R), 1.0 / NZ, f32)
    load_q.wait()
    load_m.wait()
    ls[...] = jnp.dot(m[...], factor(0), preferred_element_type=f32).astype(bf16)
    pl.semaphore_wait(barrier, NY + NZ + NX - 2)

    def chunk(j):
        return pl.ds(pl.multiple_of(lax.rem(j + 2 * NZ, NZ) * LZ, LZ), LZ)

    def ring_chunk(way, step):
        return chunk(z + 5 - step if way == 0 else z - 4 + step)

    def ring_copy(way, step):
        src = m.at[ring_chunk(way, 1)] if step == 1 else ring.at[way, step - 2]
        return copy(src, ring.at[way, step - 1], ring_s.at[way, step - 1],
                    ring_r.at[way, step - 1], at_z(1 if way == 0 else NZ - 1))

    def ring_step(step):
        for way in range(2):
            if step <= LINKS[way]:
                if step > 1:
                    ring_copy(way, step - 1).wait_recv()
                    own = m[ring_chunk(way, step), :].astype(f32)
                    ring[way, step - 2] = (ring[way, step - 2].astype(f32) + own).astype(bf16)
                ring_copy(way, step).start()

    def ring_end():
        total = m[chunk(z), :].astype(f32)
        for way in range(2):
            ring_copy(way, LINKS[way]).wait_recv()
            total = total + ring[way, LINKS[way] - 1].astype(f32)
        high = total.astype(bf16)
        ms[0:LZ, :] = high
        ms[LZ : 2 * LZ, :] = (total - high.astype(f32)).astype(bf16)

    def triangular(rows):
        return lax.dot_general(
            rows, work[:, R : 2 * R], (((1,), (1,)), ((), ())),
            preferred_element_type=f32, precision=HIGHEST,
        )

    def sums_over_z(it):
        for k in RING:
            s = lax.rem(z + k, NZ)
            copy(cz.at[it, s], cz.at[it, s], cz_s.at[k], cz_r.at[it, s], at_z(k)).wait_recv()
        total = cz[it, 0]
        for s in range(1, NZ):
            total = total + cz[it, s]
        cc[it, 0] = total
        copy(cc.at[it, 0], cc.at[it, 1], cc_s, cc_r.at[it], mate).start()

    def column_scale(it):
        copy(cc.at[it, 0], cc.at[it, 1], cc_s, cc_r.at[it], mate).wait()
        scale[...] = math.sqrt(FF) / jnp.sqrt(cc[it, 0] + cc[it, 1] + norm_eps)

    def left_first(it, start):
        for k in RING:
            t = lax.rem(y + k, NY)
            start(copy(ls.at[pl.ds(t * LY, LY)], ly.at[it, y], ly_s.at[k], ly_r.at[it, y], at_y(k)))
        ring_step(1)
        total = ls[pl.ds(y * LY, LY), :].astype(f32)
        for k in RING:
            s = lax.rem(y + k, NY)
            copy(ly.at[it, s], ly.at[it, s], ly_s.at[k], ly_r.at[it, s], at_y(k)).wait_recv()
            total = total + ly[it, s].astype(f32)
        lz[z] = total.astype(bf16)
        for k in RING:
            start(copy(lz.at[z], lz.at[z], lz_s.at[k], lz_r.at[z], at_z(k)))
        for k in RING:
            s = lax.rem(z + k, NZ)
            copy(lz.at[s], lz.at[s], lz_s.at[k], lz_r.at[s], at_z(k)).wait_recv()
        total = lz[0].astype(f32)
        for s in range(1, NZ):
            total = total + lz[s].astype(f32)
        la[it, pl.ds(y * LY, LY), :] = (total * scale[0:1, :]).astype(bf16)
        mine = la.at[it, pl.ds(y * LY, LY)]
        for k in RING:
            start(copy(mine, mine, la_s.at[k], la_r.at[it, y], at_y(k)))
        ring_step(2)
        for k in RING:
            s = lax.rem(y + k, NY)
            theirs = la.at[it, pl.ds(s * LY, LY)]
            copy(theirs, theirs, la_s.at[k], la_r.at[it, s], at_y(k)).wait_recv()

    def left_later(it, start):
        both = jnp.dot(ms[...], factor(it), preferred_element_type=f32)
        ly[it, y] = (both[0:LZ, :] + both[LZ : 2 * LZ, :]).astype(bf16)
        for k in RING:
            start(copy(ly.at[it, y], ly.at[it, y], ly_s.at[k], ly_r.at[it, y], at_y(k)))
        sums_over_z(it - 1)
        for k in RING:
            s = lax.rem(y + k, NY)
            copy(ly.at[it, s], ly.at[it, s], ly_s.at[k], ly_r.at[it, s], at_y(k)).wait_recv()
        column_scale(it - 1)
        total = ly[it, 0].astype(f32)
        for s in range(1, NY):
            total = total + ly[it, s].astype(f32)
        rows = (triangular(total) * (scale[0:1, :] * (1.0 / NZ**2))).astype(bf16)
        la[it, pl.ds(z * LZ, LZ), :] = rows
        mine = la.at[it, pl.ds(z * LZ, LZ)]
        for k in RING:
            start(copy(mine, mine, la_s.at[k], la_r.at[it, z], at_z(k)))
        return rows

    def wait_left_later(it):
        for k in RING:
            s = lax.rem(z + k, NZ)
            theirs = la.at[it, pl.ds(s * LZ, LZ)]
            copy(theirs, theirs, la_s.at[k], la_r.at[it, s], at_z(k)).wait_recv()

    def product(block, left, half):
        columns = pl.ds(pl.multiple_of(half * RC, 128), RC)
        return lax.dot_general(
            block[:, columns], left, (((0,), (0,)), ((), ())), preferred_element_type=f32
        ).reshape(NZ, RZ, R)

    def iteration(it):
        first, final = it == 0, it == ITERS - 1
        sends = []

        def start(cp):
            cp.start()
            sends.append(cp)

        def gram_to_mate():
            left = la[it]
            gs[...] = lax.dot_general(
                left, left, (((0,), (0,)), ((), ())), preferred_element_type=f32
            )
            start(copy(gs, gc.at[it], gc_s, gc_r.at[it], mate))

        def gram_over_x():
            copy(gs, gc.at[it], gc_s, gc_r.at[it], mate).wait_recv()
            gx[it, x] = (gs[...] + gc[it]).astype(bf16)
            for k in RING_X:
                start(copy(gx.at[it, x], gx.at[it, x], gx_s.at[k], gx_r.at[it, x], at_x(k)))

        def factorise():
            for k in RING_X:
                s = lax.rem(x + k, NX)
                copy(gx.at[it, s], gx.at[it, s], gx_s.at[k], gx_r.at[it, s], at_x(k)).wait_recv()
            gram = (gx[it, 0].astype(f32) + gx[it, 1].astype(f32)) + (
                gx[it, 2].astype(f32) + gx[it, 3].astype(f32)
            )
            eye = lax.broadcasted_iota(jnp.int32, (R, R), 0) == lax.broadcasted_iota(
                jnp.int32, (R, R), 1
            )
            ridge = (ridge_scale / R) * jnp.sum(jnp.where(eye, gram, 0.0), keepdims=True)
            work[:, 0:R] = jnp.where(eye, gram + ridge, gram)
            work[:, R : 2 * R] = jnp.where(eye, 1.0, 0.0)
            factor_inverse(work)

        def gather(rows):
            ra[it + 1, c, z] = rows.astype(bf16)
            mine = ra.at[it + 1, c, z]
            for k in RING:
                start(copy(mine, mine, ra_s.at[k], ra_r.at[it, z], at_z(k)))

        def squares(right):
            cy[it, y] = jnp.broadcast_to(jnp.sum(right * right, axis=0, keepdims=True), (8, R))
            for k in RING:
                start(copy(cy.at[it, y], cy.at[it, y], cy_s.at[k], cy_r.at[it, y], at_y(k)))

        def squares_over_y():
            for k in RING:
                s = lax.rem(y + k, NY)
                copy(cy.at[it, s], cy.at[it, s], cy_s.at[k], cy_r.at[it, s], at_y(k)).wait_recv()
            total = cy[it, 0]
            for s in range(1, NY):
                total = total + cy[it, s]
            cz[it, z] = total
            for k in RING:
                start(copy(cz.at[it, z], cz.at[it, z], cz_s.at[k], cz_r.at[it, z], at_z(k)))

        if first:
            left_first(it, start)
            gram_to_mate()
            block, rows = m, la[it]
        else:
            rows = left_later(it, start)
            block, rows = ms, jnp.concatenate([rows, rows], 0)

        rcs[...] = product(block, rows, 1 - c).astype(bf16)
        to_mate = copy(rcs, rc.at[it], rc_s, rc_r.at[it], mate)
        start(to_mate)
        own = product(block, rows, c)
        if first:
            gram_over_x()
        to_mate.wait_recv()
        rzs[...] = (own + rc[it].astype(f32)).astype(bf16)
        for k in RING:
            t = lax.rem(z + k, NZ)
            start(copy(rzs.at[t], rz.at[it, z], rz_s.at[k], rz_r.at[it, z], at_z(k)))
        if first:
            ring_step(3)
        else:
            wait_left_later(it)
            gram_to_mate()
            gram_over_x()

        total = rzs[z].astype(f32)
        for k in RING:
            s = lax.rem(z + k, NZ)
            copy(rz.at[it, s], rz.at[it, s], rz_s.at[k], rz_r.at[it, s], at_z(k)).wait_recv()
            total = total + rz[it, s].astype(f32)
        rx[it, x] = total.astype(bf16)
        for k in RING_X:
            start(copy(rx.at[it, x], rx.at[it, x], rx_s.at[k], rx_r.at[it, x], at_x(k)))
        if final:
            factorise()
        for k in RING_X:
            s = lax.rem(x + k, NX)
            copy(rx.at[it, s], rx.at[it, s], rx_s.at[k], rx_r.at[it, s], at_x(k)).wait_recv()
        total = (rx[it, 0].astype(f32) + rx[it, 1].astype(f32)) + (
            rx[it, 2].astype(f32) + rx[it, 3].astype(f32)
        )

        if final:
            right = triangular(total) * (1.0 / NZ)
            gather(right)
            squares(right)
            squares_over_y()
        else:
            gather(total)
            if first:
                ring_step(4)
            factorise()
            squares(triangular(total) * (1.0 / NZ))
        for k in RING:
            s = lax.rem(z + k, NZ)
            there = ra.at[it + 1, c, s]
            copy(there, there, ra_s.at[k], ra_r.at[it, s], at_z(k)).wait_recv()
        half = ra.at[it + 1, c]
        start(copy(half, half, rm_s, rm_r.at[it], mate))
        if not final:
            squares_over_y()
        if first:
            ring_end()
        half = ra.at[it + 1, 1 - c]
        copy(half, half, rm_s, rm_r.at[it], mate).wait_recv()
        for cp in sends:
            cp.wait_send()
        if first:
            for way in range(2):
                for step in range(1, LINKS[way] + 1):
                    ring_copy(way, step).wait_send()

    for it in range(ITERS):
        iteration(it)
    last = ITERS - 1
    lr_ref[...] = triangular(la[last].astype(f32)).astype(bf16)
    rr_ref[...] = factor(ITERS)
    sums_over_z(last)
    column_scale(last)
    d_ref[...] = scale[...]


def iterate(block, q):
    vmem = pl.BlockSpec(memory_space=pltpu.VMEM)
    hbm = pl.BlockSpec(memory_space=pltpu.HBM)
    dma = pltpu.SemaphoreType.DMA
    n = ITERS
    return pl.pallas_call(
        iterate_kernel,
        out_shape=[
            jax.ShapeDtypeStruct((ROWS, R), bf16),
            jax.ShapeDtypeStruct((COLS, R), bf16),
            jax.ShapeDtypeStruct((8, R), f32),
        ],
        in_specs=[hbm, hbm],
        out_specs=[vmem] * 3,
        scratch_shapes=[
            pltpu.VMEM((ROWS, COLS), bf16),
            pltpu.VMEM((2 * LZ, COLS), bf16),
            pltpu.VMEM((2, 4, LZ, COLS), bf16),
            pltpu.VMEM((ROWS, R), bf16),
            pltpu.VMEM((n, NY, LY, R), bf16),
            pltpu.VMEM((NZ, LY, R), bf16),
            pltpu.VMEM((n, ROWS, R), bf16),
            pltpu.VMEM((n, R, R), f32),
            pltpu.VMEM((n, NX, R, R), bf16),
            pltpu.VMEM((R, R), f32),
            pltpu.VMEM((R, 2 * R), f32),
            pltpu.VMEM((NZ, RZ, R), bf16),
            pltpu.VMEM((n, NZ, RZ, R), bf16),
            pltpu.VMEM((NZ, RZ, R), bf16),
            pltpu.VMEM((n, NZ, RZ, R), bf16),
            pltpu.VMEM((n, NX, RZ, R), bf16),
            pltpu.VMEM((n + 1, 2, NZ, RZ, R), bf16),
            pltpu.VMEM((n, NY, 8, R), f32),
            pltpu.VMEM((n, NZ, 8, R), f32),
            pltpu.VMEM((n, 2, 8, R), f32),
            pltpu.VMEM((8, R), f32),
            dma(()), dma(()),
            dma((2, 4)), dma((2, 4)),
            dma((NY,)), dma((n, NY)),
            dma((NZ,)), dma((NZ,)),
            dma((NY,)), dma((n, NY)),
            dma(()), dma((n,)),
            dma((NX,)), dma((n, NX)),
            dma(()), dma((n,)),
            dma((NZ,)), dma((n, NZ)),
            dma((NX,)), dma((n, NX)),
            dma((NZ,)), dma((n, NZ)),
            dma(()), dma((n,)),
            dma((NY,)), dma((n, NY)),
            dma((NZ,)), dma((n, NZ)),
            dma(()), dma((n,)),
        ],
        compiler_params=pltpu.CompilerParams(
            collective_id=0, has_side_effects=True, vmem_limit_bytes=56 << 20
        ),
        cost_estimate=pl.CostEstimate(
            flops=12 * ROWS * COLS * R, bytes_accessed=2 * ROWS * COLS, transcendentals=0
        ),
    )(block, q.reshape(2, NZ, RZ, R))


def finish_kernel(m, left, right, scale, m_out, u_out, q_out):
    correction = lax.dot_general(
        left[...], right[...], (((1,), (1,)), ((), ())), preferred_element_type=f32
    )
    m_out[...] = (m[...].astype(f32) - (1.0 - momentum_decay) * correction).astype(bf16)
    u_out[...] = math.sqrt(D) * left[...].astype(f32)

    @pl.when(pl.program_id(0) == 0)
    def _():
        q_out[...] = (right[...].astype(f32) * scale[0:1, :]).astype(bf16)


def finish(block, left, right, scale):
    steps = 2
    rows = ROWS // steps
    return pl.pallas_call(
        finish_kernel,
        grid=(steps,),
        out_shape=[
            jax.ShapeDtypeStruct((ROWS, COLS), bf16),
            jax.ShapeDtypeStruct((ROWS, R), f32),
            jax.ShapeDtypeStruct((COLS, R), bf16),
        ],
        in_specs=[
            pl.BlockSpec((rows, COLS), lambda i: (i, 0)),
            pl.BlockSpec((rows, R), lambda i: (i, 0)),
            pl.BlockSpec((COLS, R), lambda i: (0, 0)),
            pl.BlockSpec((8, R), lambda i: (0, 0)),
        ],
        out_specs=[
            pl.BlockSpec((rows, COLS), lambda i: (i, 0)),
            pl.BlockSpec((rows, R), lambda i: (i, 0)),
            pl.BlockSpec((COLS, R), lambda i: (0, 0)),
        ],
        compiler_params=pltpu.CompilerParams(vmem_limit_bytes=56 << 20),
        cost_estimate=pl.CostEstimate(
            flops=2 * ROWS * COLS * R, bytes_accessed=4 * ROWS * COLS, transcendentals=0
        ),
    )(block, left, right, scale)


def shards(momentum, q_prev):
    block = momentum[0]
    left, right, scale = iterate(block, q_prev)
    momentum_next, update_left, q_next = finish(block, left, right, scale)
    return momentum_next[None], update_left, q_next


def solution(mesh):
    in_specs = (P("replica", "fsdp", "tensor"), P("tensor", None))
    out_specs = (P("replica", "fsdp", "tensor"), P("fsdp", None), P("tensor", None))
    return jax.shard_map(shards, mesh=mesh, in_specs=in_specs, out_specs=out_specs, check_vma=False)
```

```python
import functools
import math

import jax
import jax.numpy as jnp
from jax import lax
from jax.experimental import pallas as pl
from jax.experimental.pallas import tpu as pltpu
from jax.sharding import PartitionSpec as P

D = 4096
FF = 14336
R = 128
ITERS = 3
NY, NZ, NX = 8, 8, 4
ROWS = 512
COLS = 1792
LY = ROWS // NY
HALF = 128
CZ = 2 * HALF
PAD = NZ * CZ
LINKS = (4, 3)
RING = (4, 3, 5, 2, 6, 1, 7)
RING_X = (2, 1, 3)
PLACES = "ABCD"

ridge_scale = 1e-06
norm_eps = 1e-06
momentum_decay = 0.95

MESH = pl.DeviceIdType.MESH
f32, bf16 = jnp.float32, jnp.bfloat16
HIGHEST = lax.Precision.HIGHEST


def split3(w):
    high = w.astype(bf16).astype(f32)
    rest = w - high
    mid = rest.astype(bf16).astype(f32)
    return high, mid, rest - mid


def factor_inverse(work):
    size = 16
    sub = lax.broadcasted_iota(jnp.int32, (size, R), 0)
    lane = lax.broadcasted_iota(jnp.int32, (size, R), 1)
    for first in range(0, R, size):
        left, right = work[first : first + size, 0:R], work[first : first + size, R : 2 * R]
        cols = [
            jnp.broadcast_to(left[:, first + k : first + k + 1], (size, R)) for k in range(size)
        ]
        scale = jnp.zeros((size, R), f32)
        for j in range(size):
            pivot = jnp.broadcast_to(cols[j][j : j + 1, :], (size, R))
            scale = jnp.where(sub == j, lax.rsqrt(pivot), scale)
            if j < size - 1:
                ratio = jnp.where(sub > j, cols[j], 0.0) * (1.0 / pivot)
                for k in range(j + 1, size):
                    cols[k] = cols[k] - ratio * cols[k][j : j + 1, :]
                left = left - ratio * left[j : j + 1, :]
                right = right - ratio * right[j : j + 1, :]
        left = jnp.where(lane >= first, left * scale, 0.0)
        right = right * scale
        work[first : first + size, 0:R] = left
        work[first : first + size, R : 2 * R] = right
        below = first + size
        if below < R:
            ph, pm, pw = split3(jnp.concatenate([left, right], 1))
            wh, wm, ww = split3(jnp.where(lane >= below, left, 0.0))
            a = jnp.concatenate([wh, wh, wm, wm, wh, ww], 0).astype(bf16)
            b = jnp.concatenate([ph, pm, ph, pm, pw, ph], 0).astype(bf16)
            update = lax.dot_general(a, b, (((0,), (0,)), ((), ())), preferred_element_type=f32)
            work[below:R, :] = work[below:R, :] - update[below:R, :]


def iterate_kernel(
    m_hbm, q_hbm, lr_ref, rr_ref, d_ref,
    m, q, ms, ring, ls, ly, lz, la, gc, gx, gs, work, rcs, rc, rzs, rz, r2, r2s, r2c, rx, ra, rf,
    cy, cz, cc, m_sem, q_sem, ring_s, ring_r, ly_s, ly_r, lz_s, lz_r, la_s, la_r, gc_s, gc_r,
    gx_s, gx_r, rc_s, rc_r, rz_s, rz_r, rx_s, rx_r, ra_s, ra_r, rf_s, rf_r, rm_s, rm_r,
    cy_s, cy_r, cz_s, cz_r, cc_s, cc_r,
):
    z, fs, y = lax.axis_index("replica"), lax.axis_index("fsdp"), lax.axis_index("tensor")
    x, c = fs // 2, lax.rem(fs, 2)
    mate = {"fsdp": x * 2 + 1 - c}

    def at_y(k):
        return {"tensor": lax.rem(y + k, NY)}

    def at_z(k):
        return {"replica": lax.rem(z + k, NZ)}

    def at_x(k):
        return {"fsdp": lax.rem(x + k, NX) * 2 + c}

    def copy(src, dst, send, recv, to):
        return pltpu.make_async_remote_copy(
            src_ref=src, dst_ref=dst, send_sem=send, recv_sem=recv, device_id=to, device_id_type=MESH
        )

    barrier = pltpu.get_barrier_semaphore()
    for k in RING:
        pl.semaphore_signal(barrier, inc=1, device_id=at_y(k), device_id_type=MESH)
        pl.semaphore_signal(barrier, inc=1, device_id=at_z(k), device_id_type=MESH)
    for k in RING_X:
        pl.semaphore_signal(barrier, inc=1, device_id=at_x(k), device_id_type=MESH)
    pl.semaphore_signal(barrier, inc=1, device_id=mate, device_id_type=MESH)
    load_m = pltpu.make_async_copy(m_hbm, m.at[:, pl.ds(0, COLS)], m_sem)
    load_m.start()
    load_q = pltpu.make_async_copy(q_hbm, q, q_sem)
    load_q.start()
    m[:, COLS:PAD] = jnp.zeros((ROWS, PAD - COLS), bf16)
    load_q.wait()
    load_m.wait()
    ls[0] = jnp.dot(m[:, 0:COLS], q[...], preferred_element_type=f32).astype(bf16)
    pl.semaphore_wait(barrier, NY + NZ + NX - 2)

    def chunk(j):
        return pl.ds(pl.multiple_of(lax.rem(j + 2 * NZ, NZ) * CZ, CZ), CZ)

    def ring_chunk(way, step):
        return chunk(z + 5 - step if way == 0 else z - 4 + step)

    def ring_copy(way, step):
        src = m.at[:, ring_chunk(way, 1)] if step == 1 else ring.at[way, step - 2]
        return copy(src, ring.at[way, step - 1], ring_s.at[way, step - 1],
                    ring_r.at[way, step - 1], at_z(1 if way == 0 else NZ - 1))

    def ring_step(step):
        for way in range(2):
            if step <= LINKS[way]:
                if step > 1:
                    ring_copy(way, step - 1).wait_recv()
                    own = m[:, ring_chunk(way, step)].astype(f32)
                    ring[way, step - 2] = (ring[way, step - 2].astype(f32) + own).astype(bf16)
                ring_copy(way, step).start()

    def ring_end():
        total = m[:, chunk(z)].astype(f32)
        for way in range(2):
            ring_copy(way, LINKS[way]).wait_recv()
            total = total + ring[way, LINKS[way] - 1].astype(f32)
        high = total.astype(bf16)
        ms[:, 0:CZ] = high
        ms[:, CZ : 2 * CZ] = (total - high.astype(f32)).astype(bf16)

    sends = []

    def start(cp):
        cp.start()
        sends.append(cp)

    def wait_sends():
        for cp in sends:
            cp.wait_send()
        sends.clear()

    def triangular(rows):
        return lax.dot_general(
            rows, work[:, R : 2 * R], (((1,), (1,)), ((), ())),
            preferred_element_type=f32, precision=HIGHEST,
        )

    def squares(it, right):
        cy[it, y] = jnp.broadcast_to(jnp.sum(right * right, axis=0, keepdims=True), (8, R))
        for k in RING:
            start(copy(cy.at[it, y], cy.at[it, y], cy_s.at[k], cy_r.at[it, y], at_y(k)))

    def squares_over_y(it):
        for k in RING:
            s = lax.rem(y + k, NY)
            copy(cy.at[it, s], cy.at[it, s], cy_s.at[k], cy_r.at[it, s], at_y(k)).wait_recv()
        total = cy[it, 0]
        for s in range(1, NY):
            total = total + cy[it, s]
        cz[it, z] = total
        for k in RING:
            start(copy(cz.at[it, z], cz.at[it, z], cz_s.at[k], cz_r.at[it, z], at_z(k)))

    def squares_over_z(it):
        for k in RING:
            s = lax.rem(z + k, NZ)
            copy(cz.at[it, s], cz.at[it, s], cz_s.at[k], cz_r.at[it, s], at_z(k)).wait_recv()
        total = cz[it, 0]
        for s in range(1, NZ):
            total = total + cz[it, s]
        cc[it, 0] = total
        start(copy(cc.at[it, 0], cc.at[it, 1], cc_s, cc_r.at[it], mate))

    def column_scale(it):
        copy(cc.at[it, 0], cc.at[it, 1], cc_s, cc_r.at[it], mate).wait_recv()
        return math.sqrt(FF) / jnp.sqrt(cc[it, 0] + cc[it, 1] + norm_eps)

    def factorise(it):
        for k in RING_X:
            s = lax.rem(x + k, NX)
            copy(gx.at[it, s], gx.at[it, s], gx_s.at[k], gx_r.at[it, s], at_x(k)).wait_recv()
        gram = (gx[it, 0].astype(f32) + gx[it, 1].astype(f32)) + (
            gx[it, 2].astype(f32) + gx[it, 3].astype(f32)
        )
        if it > 0:
            scale = jnp.broadcast_to(column_scale(it - 1)[0:1, :], (R, R))
            gram = gram * scale * scale.T
        eye = lax.broadcasted_iota(jnp.int32, (R, R), 0) == lax.broadcasted_iota(
            jnp.int32, (R, R), 1
        )
        ridge = (ridge_scale / R) * jnp.sum(jnp.where(eye, gram, 0.0), keepdims=True)
        work[:, 0:R] = jnp.where(eye, gram + ridge, gram)
        work[:, R : 2 * R] = jnp.where(eye, 1.0, 0.0)
        factor_inverse(work)
        if it > 0:
            work[:, R : 2 * R] = work[:, R : 2 * R] * scale

    def right_total(it):
        return (rx[it, 0].astype(f32) + rx[it, 1].astype(f32)) + (
            rx[it, 2].astype(f32) + rx[it, 3].astype(f32)
        )

    def left_factor(it):
        if it > 0:
            there = ra.at[it - 1, 1 - c]
            copy(there, there, ra_s, ra_r.at[it - 1], mate).wait_recv()
            rows = ra[it - 1].reshape(CZ, R)
            if it == 1:
                ring_end()
            ls[it] = jnp.dot(
                ms[...], jnp.concatenate([rows, rows], 0), preferred_element_type=f32
            ).astype(bf16)
        for k in RING:
            t = lax.rem(y + k, NY)
            start(copy(ls.at[it, pl.ds(t * LY, LY)], ly.at[it, y], ly_s.at[k], ly_r.at[it, y], at_y(k)))
        if it > 0:
            factorise(it - 1)
            squares(it - 1, triangular(right_total(it - 1)) * (1.0 / NZ))
        ring_at(it, "A")
        total = ls[it, pl.ds(y * LY, LY), :].astype(f32)
        for k in RING:
            s = lax.rem(y + k, NY)
            copy(ly.at[it, s], ly.at[it, s], ly_s.at[k], ly_r.at[it, s], at_y(k)).wait_recv()
            total = total + ly[it, s].astype(f32)
        lz[it, z] = total.astype(bf16)
        for k in RING:
            start(copy(lz.at[it, z], lz.at[it, z], lz_s.at[k], lz_r.at[it, z], at_z(k)))
        if it > 0:
            squares_over_y(it - 1)
        ring_at(it, "B")
        for k in RING:
            s = lax.rem(z + k, NZ)
            copy(lz.at[it, s], lz.at[it, s], lz_s.at[k], lz_r.at[it, s], at_z(k)).wait_recv()
        total = lz[it, 0].astype(f32)
        for s in range(1, NZ):
            total = total + lz[it, s].astype(f32)
        total = total * (1.0 / NZ) if it == 0 else triangular(total) * (1.0 / NZ**2)
        la[it, pl.ds(y * LY, LY), :] = total.astype(bf16)
        mine = la.at[it, pl.ds(y * LY, LY)]
        for k in RING:
            start(copy(mine, mine, la_s.at[k], la_r.at[it, y], at_y(k)))
        if it > 0:
            squares_over_z(it - 1)
        ring_at(it, "C")
        for k in RING:
            s = lax.rem(y + k, NY)
            theirs = la.at[it, pl.ds(s * LY, LY)]
            copy(theirs, theirs, la_s.at[k], la_r.at[it, s], at_y(k)).wait_recv()

    def ring_at(it, point):
        if it == 0 and point in PLACES:
            ring_step(PLACES.index(point) + 1)

    def right_factor(it):
        left = la[it]
        gs[it] = lax.dot_general(left, left, (((0,), (0,)), ((), ())), preferred_element_type=f32)
        start(copy(gs.at[it], gc.at[it], gc_s, gc_r.at[it], mate))
        if it == 0:
            rcs[...] = (
                lax.dot_general(m[...], left, (((0,), (0,)), ((), ())), preferred_element_type=f32)
                .astype(bf16)
                .reshape(NZ, 2, HALF, R)
            )
            to_mate = copy(rcs.at[:, 1 - c], rc, rc_s, rc_r.at[it], mate)
        else:
            both = lax.dot_general(ms[...], left, (((0,), (0,)), ((), ())), preferred_element_type=f32)
            both = (both[0:CZ, :] + both[CZ : 2 * CZ, :]).reshape(2, HALF, R)
            r2[...] = both
            r2s[it] = both.astype(bf16)
            to_mate = copy(r2s.at[it, 1 - c], r2c.at[it], rc_s, rc_r.at[it], mate)
        start(to_mate)
        copy(gs.at[it], gc.at[it], gc_s, gc_r.at[it], mate).wait_recv()
        gx[it, x] = (gs[it] + gc[it]).astype(bf16)
        for k in RING_X:
            start(copy(gx.at[it, x], gx.at[it, x], gx_s.at[k], gx_r.at[it, x], at_x(k)))
        to_mate.wait_recv()
        if it == 0:
            rzs[...] = (rcs[:, c].astype(f32) + rc[...].astype(f32)).astype(bf16)
            for k in RING:
                t = lax.rem(z + k, NZ)
                start(copy(rzs.at[t], rz.at[z], rz_s.at[k], rz_r.at[z], at_z(k)))
            ring_at(it, "D")
            total = rzs[z].astype(f32)
            for k in RING:
                s = lax.rem(z + k, NZ)
                copy(rz.at[s], rz.at[s], rz_s.at[k], rz_r.at[s], at_z(k)).wait_recv()
                total = total + rz[s].astype(f32)
        else:
            total = r2[c] + r2c[it].astype(f32)
        rx[it, x] = total.astype(bf16)
        for k in RING_X:
            start(copy(rx.at[it, x], rx.at[it, x], rx_s.at[k], rx_r.at[it, x], at_x(k)))
        ring_at(it, "E")
        if it == ITERS - 1:
            factorise(it)
        for k in RING_X:
            s = lax.rem(x + k, NX)
            copy(rx.at[it, s], rx.at[it, s], rx_s.at[k], rx_r.at[it, s], at_x(k)).wait_recv()

    last = ITERS - 1
    for it in range(ITERS):
        left_factor(it)
        right_factor(it)
        if it < last:
            wait_sends()
            ra[it, c] = right_total(it).astype(bf16)
            start(copy(ra.at[it, c], ra.at[it, c], ra_s, ra_r.at[it], mate))

    right = triangular(right_total(last)) * (1.0 / NZ)
    squares(last, right)
    rf[z, c] = right.astype(bf16)
    mine = rf.at[z, c]
    for k in RING:
        start(copy(mine, mine, rf_s.at[k], rf_r.at[z], at_z(k)))
    lr_ref[...] = triangular(la[last].astype(f32)).astype(bf16)
    squares_over_y(last)
    for k in RING:
        s = lax.rem(z + k, NZ)
        there = rf.at[s, c]
        copy(there, there, rf_s.at[k], rf_r.at[s], at_z(k)).wait_recv()
    half = rf.at[:, c]
    start(copy(half, half, rm_s, rm_r, mate))
    squares_over_z(last)
    half = rf.at[:, 1 - c]
    copy(half, half, rm_s, rm_r, mate).wait_recv()
    rr_ref[...] = rf[...].reshape(PAD, R)[0:COLS, :]
    d_ref[...] = column_scale(last)
    wait_sends()
    for way in range(2):
        for step in range(1, LINKS[way] + 1):
            ring_copy(way, step).wait_send()


def iterate(block, q):
    vmem = pl.BlockSpec(memory_space=pltpu.VMEM)
    hbm = pl.BlockSpec(memory_space=pltpu.HBM)
    dma = pltpu.SemaphoreType.DMA
    n = ITERS
    return pl.pallas_call(
        iterate_kernel,
        out_shape=[
            jax.ShapeDtypeStruct((ROWS, R), bf16),
            jax.ShapeDtypeStruct((COLS, R), bf16),
            jax.ShapeDtypeStruct((8, R), f32),
        ],
        in_specs=[hbm, hbm],
        out_specs=[vmem] * 3,
        scratch_shapes=[
            pltpu.VMEM((ROWS, PAD), bf16),
            pltpu.VMEM((COLS, R), bf16),
            pltpu.VMEM((ROWS, 2 * CZ), bf16),
            pltpu.VMEM((2, 4, ROWS, CZ), bf16),
            pltpu.VMEM((n, ROWS, R), bf16),
            pltpu.VMEM((n, NY, LY, R), bf16),
            pltpu.VMEM((n, NZ, LY, R), bf16),
            pltpu.VMEM((n, ROWS, R), bf16),
            pltpu.VMEM((n, R, R), f32),
            pltpu.VMEM((n, NX, R, R), bf16),
            pltpu.VMEM((n, R, R), f32),
            pltpu.VMEM((R, 2 * R), f32),
            pltpu.VMEM((NZ, 2, HALF, R), bf16),
            pltpu.VMEM((NZ, HALF, R), bf16),
            pltpu.VMEM((NZ, HALF, R), bf16),
            pltpu.VMEM((NZ, HALF, R), bf16),
            pltpu.VMEM((2, HALF, R), f32),
            pltpu.VMEM((n, 2, HALF, R), bf16),
            pltpu.VMEM((n, HALF, R), bf16),
            pltpu.VMEM((n, NX, HALF, R), bf16),
            pltpu.VMEM((n, 2, HALF, R), bf16),
            pltpu.VMEM((NZ, 2, HALF, R), bf16),
            pltpu.VMEM((n, NY, 8, R), f32),
            pltpu.VMEM((n, NZ, 8, R), f32),
            pltpu.VMEM((n, 2, 8, R), f32),
            dma(()), dma(()),
            dma((2, 4)), dma((2, 4)),
            dma((NY,)), dma((n, NY)),
            dma((NZ,)), dma((n, NZ)),
            dma((NY,)), dma((n, NY)),
            dma(()), dma((n,)),
            dma((NX,)), dma((n, NX)),
            dma(()), dma((n,)),
            dma((NZ,)), dma((NZ,)),
            dma((NX,)), dma((n, NX)),
            dma(()), dma((n,)),
            dma((NZ,)), dma((NZ,)),
            dma(()), dma(()),
            dma((NY,)), dma((n, NY)),
            dma((NZ,)), dma((n, NZ)),
            dma(()), dma((n,)),
        ],
        compiler_params=pltpu.CompilerParams(
            collective_id=0, has_side_effects=True, vmem_limit_bytes=56 << 20
        ),
        cost_estimate=pl.CostEstimate(
            flops=12 * ROWS * COLS * R, bytes_accessed=2 * ROWS * COLS, transcendentals=0
        ),
    )(block, q)


def finish_kernel(m, left, right, scale, m_out, u_out, q_out):
    correction = lax.dot_general(
        left[...], right[...], (((1,), (1,)), ((), ())), preferred_element_type=f32
    )
    m_out[...] = (m[...].astype(f32) - (1.0 - momentum_decay) * correction).astype(bf16)
    u_out[...] = math.sqrt(D) * left[...].astype(f32)

    @pl.when(pl.program_id(0) == 0)
    def _():
        q_out[...] = (right[...].astype(f32) * scale[0:1, :]).astype(bf16)


def finish(block, left, right, scale):
    steps = 2
    rows = ROWS // steps
    return pl.pallas_call(
        finish_kernel,
        grid=(steps,),
        out_shape=[
            jax.ShapeDtypeStruct((ROWS, COLS), bf16),
            jax.ShapeDtypeStruct((ROWS, R), f32),
            jax.ShapeDtypeStruct((COLS, R), bf16),
        ],
        in_specs=[
            pl.BlockSpec((rows, COLS), lambda i: (i, 0)),
            pl.BlockSpec((rows, R), lambda i: (i, 0)),
            pl.BlockSpec((COLS, R), lambda i: (0, 0)),
            pl.BlockSpec((8, R), lambda i: (0, 0)),
        ],
        out_specs=[
            pl.BlockSpec((rows, COLS), lambda i: (i, 0)),
            pl.BlockSpec((rows, R), lambda i: (i, 0)),
            pl.BlockSpec((COLS, R), lambda i: (0, 0)),
        ],
        compiler_params=pltpu.CompilerParams(vmem_limit_bytes=56 << 20),
        cost_estimate=pl.CostEstimate(
            flops=2 * ROWS * COLS * R, bytes_accessed=4 * ROWS * COLS, transcendentals=0
        ),
    )(block, left, right, scale)


def shards(momentum, q_prev):
    block = momentum[0]
    left, right, scale = iterate(block, q_prev)
    momentum_next, update_left, q_next = finish(block, left, right, scale)
    return momentum_next[None], update_left, q_next


def solution(mesh):
    in_specs = (P("replica", "fsdp", "tensor"), P("tensor", None))
    out_specs = (P("replica", "fsdp", "tensor"), P("fsdp", None), P("tensor", None))
    return jax.shard_map(shards, mesh=mesh, in_specs=in_specs, out_specs=out_specs, check_vma=False)
```

```python
import functools
import math

import jax
import jax.numpy as jnp
from jax import lax
from jax.experimental import pallas as pl
from jax.experimental.pallas import tpu as pltpu
from jax.sharding import PartitionSpec as P

D = 4096
FF = 14336
R = 128
ITERS = 3
NY, NZ, NX = 8, 8, 4
ROWS = 512
COLS = 1792
LY = ROWS // NY
HALF = 128
CZ = 2 * HALF
PAD = NZ * CZ
LS = LY // 2
LOADS = 4
LINKS = (4, 3)
RING = (4, 3, 5, 2, 6, 1, 7)
RING_X = (2, 1, 3)
PLACES = "ABCD"

ridge_scale = 1e-06
norm_eps = 1e-06
momentum_decay = 0.95

MESH = pl.DeviceIdType.MESH
f32, bf16 = jnp.float32, jnp.bfloat16
HIGHEST = lax.Precision.HIGHEST


def split3(w):
    high = w.astype(bf16).astype(f32)
    rest = w - high
    mid = rest.astype(bf16).astype(f32)
    return high, mid, rest - mid


def factor_inverse(work):
    size = 16
    sub = lax.broadcasted_iota(jnp.int32, (size, R), 0)
    lane = lax.broadcasted_iota(jnp.int32, (size, R), 1)
    for first in range(0, R, size):
        left, right = work[first : first + size, 0:R], work[first : first + size, R : 2 * R]
        cols = [
            jnp.broadcast_to(left[:, first + k : first + k + 1], (size, R)) for k in range(size)
        ]
        scale = jnp.zeros((size, R), f32)
        for j in range(size):
            pivot = jnp.broadcast_to(cols[j][j : j + 1, :], (size, R))
            scale = jnp.where(sub == j, lax.rsqrt(pivot), scale)
            if j < size - 1:
                ratio = jnp.where(sub > j, cols[j], 0.0) * (1.0 / pivot)
                for k in range(j + 1, size):
                    cols[k] = cols[k] - ratio * cols[k][j : j + 1, :]
                left = left - ratio * left[j : j + 1, :]
                right = right - ratio * right[j : j + 1, :]
        left = jnp.where(lane >= first, left * scale, 0.0)
        right = right * scale
        work[first : first + size, 0:R] = left
        work[first : first + size, R : 2 * R] = right
        below = first + size
        if below < R:
            ph, pm, pw = split3(jnp.concatenate([left, right], 1))
            wh, wm, ww = split3(jnp.where(lane >= below, left, 0.0))
            a = jnp.concatenate([wh, wh, wm, wm, wh, ww], 0).astype(bf16)
            b = jnp.concatenate([ph, pm, ph, pm, pw, ph], 0).astype(bf16)
            update = lax.dot_general(a, b, (((0,), (0,)), ((), ())), preferred_element_type=f32)
            work[below:R, :] = work[below:R, :] - update[below:R, :]


def iterate_kernel(
    m_hbm, q_hbm, lr_ref, rr_ref, d_ref,
    m, q, ms, ring, ls, ly, lz, p1, p2, la, gc, gx, gs, work, rcs, rc, ro, rzs, rz, r2, r2s, r2c, rx, ra, rf, rfm,
    cy, cz, column_sq, m_sem, q_sem, ring_s, ring_r, ly_s, ly_r, lz_s, lz_r, p1_s, p1_r, p2_s, p2_r, la_s, la_r, gc_s, gc_r,
    gx_s, gx_r, rc_s, rc_r, rz_s, rz_r, rx_s, rx_r, ra_s, ra_r, rf_s, rf_r, rm_s, rm_r,
    cy_s, cy_r, cz_s, cz_r,
):
    z, fs, y = lax.axis_index("replica"), lax.axis_index("fsdp"), lax.axis_index("tensor")
    x, c = fs // 2, lax.rem(fs, 2)
    mate = {"fsdp": x * 2 + 1 - c}

    def at_y(k):
        return {"tensor": lax.rem(y + k, NY)}

    def at_z(k):
        return {"replica": lax.rem(z + k, NZ)}

    def at_x(k):
        return {"fsdp": lax.rem(x + k, NX) * 2 + c}

    def copy(src, dst, send, recv, to):
        return pltpu.make_async_remote_copy(
            src_ref=src, dst_ref=dst, send_sem=send, recv_sem=recv, device_id=to, device_id_type=MESH
        )

    barrier = pltpu.get_barrier_semaphore()
    for k in RING:
        pl.semaphore_signal(barrier, inc=1, device_id=at_y(k), device_id_type=MESH)
        pl.semaphore_signal(barrier, inc=1, device_id=at_z(k), device_id_type=MESH)
    for k in RING_X:
        pl.semaphore_signal(barrier, inc=1, device_id=at_x(k), device_id_type=MESH)
    pl.semaphore_signal(barrier, inc=1, device_id=mate, device_id_type=MESH)
    load_q = pltpu.make_async_copy(q_hbm, q, q_sem)
    load_q.start()
    block = ROWS // LOADS
    loads = []
    for k in range(LOADS):
        rows = pl.ds(k * block, block)
        loads.append(pltpu.make_async_copy(m_hbm.at[rows], m.at[rows, pl.ds(0, COLS)], m_sem.at[k]))
        loads[k].start()
    m[:, COLS:PAD] = jnp.zeros((ROWS, PAD - COLS), bf16)
    load_q.wait()
    for k in range(LOADS):
        rows = slice(k * block, (k + 1) * block)
        loads[k].wait()
        ls[0, rows, :] = jnp.dot(
            m[rows, 0:COLS], q[...], preferred_element_type=f32
        ).astype(bf16)
    pl.semaphore_wait(barrier, NY + NZ + NX - 2)

    def chunk(j):
        return pl.ds(pl.multiple_of(lax.rem(j + 2 * NZ, NZ) * CZ, CZ), CZ)

    def ring_chunk(way, step):
        return chunk(z + 5 - step if way == 0 else z - 4 + step)

    def ring_copy(way, step):
        src = m.at[:, ring_chunk(way, 1)] if step == 1 else ring.at[way, step - 2]
        return copy(src, ring.at[way, step - 1], ring_s.at[way, step - 1],
                    ring_r.at[way, step - 1], at_z(1 if way == 0 else NZ - 1))

    def ring_step(step):
        for way in range(2):
            if step <= LINKS[way]:
                if step > 1:
                    ring_copy(way, step - 1).wait_recv()
                    own = m[:, ring_chunk(way, step)].astype(f32)
                    ring[way, step - 2] = (ring[way, step - 2].astype(f32) + own).astype(bf16)
                ring_copy(way, step).start()

    def ring_end():
        total = m[:, chunk(z)].astype(f32)
        for way in range(2):
            ring_copy(way, LINKS[way]).wait_recv()
            total = total + ring[way, LINKS[way] - 1].astype(f32)
        high = total.astype(bf16)
        ms[:, 0:CZ] = high
        ms[:, CZ : 2 * CZ] = (total - high.astype(f32)).astype(bf16)

    sends = []

    def start(cp):
        cp.start()
        sends.append(cp)

    def wait_sends():
        for cp in sends:
            cp.wait_send()
        sends.clear()

    def triangular(rows):
        return lax.dot_general(
            rows, work[:, R : 2 * R], (((1,), (1,)), ((), ())),
            preferred_element_type=f32, precision=HIGHEST,
        )

    def squares(it, right):
        cy[it, y] = jnp.broadcast_to(jnp.sum(right * right, axis=0, keepdims=True), (8, R))
        for k in RING:
            start(copy(cy.at[it, y], cy.at[it, y], cy_s.at[k], cy_r.at[it, y], at_y(k)))

    def squares_over_y(it):
        for k in RING:
            s = lax.rem(y + k, NY)
            copy(cy.at[it, s], cy.at[it, s], cy_s.at[k], cy_r.at[it, s], at_y(k)).wait_recv()
        total = cy[it, 0]
        for s in range(1, NY):
            total = total + cy[it, s]
        cz[it, z] = total
        for k in RING:
            start(copy(cz.at[it, z], cz.at[it, z], cz_s.at[k], cz_r.at[it, z], at_z(k)))

    def squares_over_z(it):
        for k in RING:
            s = lax.rem(z + k, NZ)
            copy(cz.at[it, s], cz.at[it, s], cz_s.at[k], cz_r.at[it, s], at_z(k)).wait_recv()
        total = cz[it, 0]
        for s in range(1, NZ):
            total = total + cz[it, s]
        column_sq[it] = total

    def column_scale(it):
        return math.sqrt(FF) / jnp.sqrt(column_sq[it] + norm_eps)

    def factorise(it):
        for k in RING_X:
            s = lax.rem(x + k, NX)
            copy(gx.at[it, s], gx.at[it, s], gx_s.at[k], gx_r.at[it, s], at_x(k)).wait_recv()
        gram = (gx[it, 0].astype(f32) + gx[it, 1].astype(f32)) + (
            gx[it, 2].astype(f32) + gx[it, 3].astype(f32)
        )
        if it > 0:
            scale = jnp.broadcast_to(column_scale(it - 1)[0:1, :], (R, R))
            gram = gram * scale * scale.T
        eye = lax.broadcasted_iota(jnp.int32, (R, R), 0) == lax.broadcasted_iota(
            jnp.int32, (R, R), 1
        )
        ridge = (ridge_scale / R) * jnp.sum(jnp.where(eye, gram, 0.0), keepdims=True)
        work[:, 0:R] = jnp.where(eye, gram + ridge, gram)
        work[:, R : 2 * R] = jnp.where(eye, 1.0, 0.0)
        factor_inverse(work)
        if it > 0:
            work[:, R : 2 * R] = work[:, R : 2 * R] * scale

    def right_total(it):
        return (rx[it, 0].astype(f32) + rx[it, 1].astype(f32)) + (
            rx[it, 2].astype(f32) + rx[it, 3].astype(f32)
        )

    def right_raw(it):
        return ra[it].reshape(CZ, R)

    def left_factor():
        for k in RING:
            t = lax.rem(y + k, NY)
            start(copy(ls.at[0, pl.ds(t * LY, LY)], ly.at[y], ly_s.at[k], ly_r.at[y], at_y(k)))
        ring_at(0, "A")
        total = ls[0, pl.ds(y * LY, LY), :].astype(f32)
        for k in RING:
            s = lax.rem(y + k, NY)
            copy(ly.at[s], ly.at[s], ly_s.at[k], ly_r.at[s], at_y(k)).wait_recv()
            total = total + ly[s].astype(f32)
        lz[z] = total.astype(bf16)
        for k in RING:
            start(copy(lz.at[z], lz.at[z], lz_s.at[k], lz_r.at[z], at_z(k)))
        ring_at(0, "B")
        for k in RING:
            s = lax.rem(z + k, NZ)
            copy(lz.at[s], lz.at[s], lz_s.at[k], lz_r.at[s], at_z(k)).wait_recv()
        total = lz[0].astype(f32)
        for s in range(1, NZ):
            total = total + lz[s].astype(f32)
        la[0, pl.ds(y * LY, LY), :] = (total * (1.0 / NZ)).astype(bf16)
        mine = la.at[0, pl.ds(y * LY, LY)]
        for k in RING:
            start(copy(mine, mine, la_s.at[0, k], la_r.at[0, 0, y], at_y(k)))
        ring_at(0, "C")
        for k in RING:
            s = lax.rem(y + k, NY)
            theirs = la.at[0, pl.ds(s * LY, LY)]
            copy(theirs, theirs, la_s.at[0, k], la_r.at[0, 0, s], at_y(k)).wait_recv()

    def left_halves(it):
        there = ra.at[it - 1, 1 - c]
        copy(there, there, ra_s, ra_r.at[it - 1], mate).wait_recv()
        rows = right_raw(it - 1)
        if it == 1:
            ring_end()
        ls[it] = jnp.dot(
            ms[...], jnp.concatenate([rows, rows], 0), preferred_element_type=f32
        ).astype(bf16)

        def ours(half, k):
            return pl.ds(lax.rem((z if half else y) + k, NZ) * LS + half * (ROWS // 2), LS)

        def other(half, k):
            return at_z(k) if half else at_y(k)

        me = (y, z)
        for k in RING:
            for half in range(2):
                start(copy(ls.at[it, ours(half, k)], p1.at[it, half, me[half]],
                           p1_s.at[half, k], p1_r.at[it, half, me[half]], other(half, k)))
        factorise(it - 1)
        squares(it - 1, triangular(right_raw(it - 1).astype(f32)) * (1.0 / NZ))
        totals = [ls[it, ours(half, 0), :].astype(f32) for half in range(2)]
        for k in RING:
            for half in range(2):
                s = lax.rem(me[half] + k, NZ)
                there = p1.at[it, half, s]
                copy(there, there, p1_s.at[half, k], p1_r.at[it, half, s], other(half, k)).wait_recv()
                totals[half] = totals[half] + p1[it, half, s].astype(f32)
        for half in range(2):
            p2[it, half, me[1 - half]] = totals[half].astype(bf16)
        for k in RING:
            for half in range(2):
                mine = p2.at[it, half, me[1 - half]]
                start(copy(mine, mine, p2_s.at[half, k], p2_r.at[it, half, me[1 - half]],
                           other(1 - half, k)))
        squares_over_y(it - 1)
        for k in RING:
            for half in range(2):
                s = lax.rem(me[1 - half] + k, NZ)
                there = p2.at[it, half, s]
                copy(there, there, p2_s.at[half, k], p2_r.at[it, half, s], other(1 - half, k)).wait_recv()
        totals = []
        for half in range(2):
            total = p2[it, half, 0].astype(f32)
            for s in range(1, NZ):
                total = total + p2[it, half, s].astype(f32)
            totals.append(total)
        total = triangular(jnp.concatenate(totals, 0)) * (1.0 / NZ**2)
        for half in range(2):
            la[it, ours(half, 0), :] = total[half * LS : (half + 1) * LS, :].astype(bf16)
        for k in RING:
            for half in range(2):
                mine = la.at[it, ours(half, 0)]
                start(copy(mine, mine, la_s.at[half, k], la_r.at[it, half, me[half]], other(half, k)))
        squares_over_z(it - 1)
        for k in RING:
            for half in range(2):
                theirs = la.at[it, ours(half, k)]
                s = lax.rem(me[half] + k, NZ)
                copy(theirs, theirs, la_s.at[half, k], la_r.at[it, half, s], other(half, k)).wait_recv()

    def ring_at(it, point):
        if it == 0 and point in PLACES:
            ring_step(PLACES.index(point) + 1)

    def product(left, k, half):
        columns = pl.ds(pl.multiple_of(k * CZ + half * HALF, HALF), HALF)
        return lax.dot_general(
            m[:, columns], left, (((0,), (0,)), ((), ())), preferred_element_type=f32
        )

    def right_factor(it):
        left = la[it]
        gs[it] = lax.dot_general(left, left, (((0,), (0,)), ((), ())), preferred_element_type=f32)
        start(copy(gs.at[it], gc.at[it], gc_s, gc_r.at[it], mate))
        if it == 0:
            for k in range(NZ):
                rcs[k] = product(left, k, 1 - c).astype(bf16)
            to_mate = copy(rcs, rc, rc_s, rc_r.at[it], mate)
        else:
            both = lax.dot_general(ms[...], left, (((0,), (0,)), ((), ())), preferred_element_type=f32)
            both = (both[0:CZ, :] + both[CZ : 2 * CZ, :]).reshape(2, HALF, R)
            r2[...] = both
            r2s[it] = both.astype(bf16)
            to_mate = copy(r2s.at[it, 1 - c], r2c.at[it], rc_s, rc_r.at[it], mate)
        start(to_mate)
        if it == 0:
            for k in range(NZ):
                ro[k] = product(left, k, c)
        copy(gs.at[it], gc.at[it], gc_s, gc_r.at[it], mate).wait_recv()
        gx[it, x] = (gs[it] + gc[it]).astype(bf16)
        for k in RING_X:
            start(copy(gx.at[it, x], gx.at[it, x], gx_s.at[k], gx_r.at[it, x], at_x(k)))
        to_mate.wait_recv()
        if it == 0:
            rzs[...] = (ro[...] + rc[...].astype(f32)).astype(bf16)
            for k in RING:
                t = lax.rem(z + k, NZ)
                start(copy(rzs.at[t], rz.at[z], rz_s.at[k], rz_r.at[z], at_z(k)))
            ring_at(it, "D")
            total = rzs[z].astype(f32)
            for k in RING:
                s = lax.rem(z + k, NZ)
                copy(rz.at[s], rz.at[s], rz_s.at[k], rz_r.at[s], at_z(k)).wait_recv()
                total = total + rz[s].astype(f32)
        else:
            total = r2[c] + r2c[it].astype(f32)
        rx[it, x] = total.astype(bf16)
        for k in RING_X:
            start(copy(rx.at[it, x], rx.at[it, x], rx_s.at[k], rx_r.at[it, x], at_x(k)))
        ring_at(it, "E")
        for k in RING_X:
            s = lax.rem(x + k, NX)
            copy(rx.at[it, s], rx.at[it, s], rx_s.at[k], rx_r.at[it, s], at_x(k)).wait_recv()

    last = ITERS - 1
    for it in range(ITERS):
        if it == 0:
            left_factor()
        else:
            left_halves(it)
        right_factor(it)
        ra[it, c] = right_total(it).astype(bf16)
        to_mate = copy(ra.at[it, c], ra.at[it, c], ra_s, ra_r.at[it], mate)
        to_mate.start()
        wait_sends()
        sends.append(to_mate)

    factorise(last)
    there = ra.at[last, 1 - c]
    copy(there, there, ra_s, ra_r.at[last], mate).wait_recv()
    right = triangular(right_raw(last).astype(f32)) * (1.0 / NZ)
    squares(last, right)
    rf[z] = right.astype(bf16).reshape(2, HALF, R)
    mine = rf.at[z, c]
    for k in RING:
        start(copy(mine, mine, rf_s.at[k], rf_r.at[z], at_z(k)))
    lr_ref[...] = triangular(la[last].astype(f32)).astype(bf16)
    squares_over_y(last)
    for k in RING:
        s = lax.rem(z + k, NZ)
        there = rf.at[s, c]
        copy(there, there, rf_s.at[k], rf_r.at[s], at_z(k)).wait_recv()
    start(copy(rf.at[:, c], rfm, rm_s, rm_r, mate))
    squares_over_z(last)
    copy(rfm, rfm, rm_s, rm_r, mate).wait_recv()
    for k in range(COLS // CZ):
        rr_ref[pl.ds(k * CZ + c * HALF, HALF), :] = rf[k, c]
        rr_ref[pl.ds(k * CZ + (1 - c) * HALF, HALF), :] = rfm[k]
    d_ref[...] = column_scale(last)
    wait_sends()
    for way in range(2):
        for step in range(1, LINKS[way] + 1):
            ring_copy(way, step).wait_send()


def iterate(block, q):
    vmem = pl.BlockSpec(memory_space=pltpu.VMEM)
    hbm = pl.BlockSpec(memory_space=pltpu.HBM)
    dma = pltpu.SemaphoreType.DMA
    n = ITERS
    return pl.pallas_call(
        iterate_kernel,
        out_shape=[
            jax.ShapeDtypeStruct((ROWS, R), bf16),
            jax.ShapeDtypeStruct((COLS, R), bf16),
            jax.ShapeDtypeStruct((8, R), f32),
        ],
        in_specs=[hbm, hbm],
        out_specs=[vmem] * 3,
        scratch_shapes=[
            pltpu.VMEM((ROWS, PAD), bf16),
            pltpu.VMEM((COLS, R), bf16),
            pltpu.VMEM((ROWS, 2 * CZ), bf16),
            pltpu.VMEM((2, 4, ROWS, CZ), bf16),
            pltpu.VMEM((n, ROWS, R), bf16),
            pltpu.VMEM((NY, LY, R), bf16),
            pltpu.VMEM((NZ, LY, R), bf16),
            pltpu.VMEM((n, 2, NY, LS, R), bf16),
            pltpu.VMEM((n, 2, NZ, LS, R), bf16),
            pltpu.VMEM((n, ROWS, R), bf16),
            pltpu.VMEM((n, R, R), f32),
            pltpu.VMEM((n, NX, R, R), bf16),
            pltpu.VMEM((n, R, R), f32),
            pltpu.VMEM((R, 2 * R), f32),
            pltpu.VMEM((NZ, HALF, R), bf16),
            pltpu.VMEM((NZ, HALF, R), bf16),
            pltpu.VMEM((NZ, HALF, R), f32),
            pltpu.VMEM((NZ, HALF, R), bf16),
            pltpu.VMEM((NZ, HALF, R), bf16),
            pltpu.VMEM((2, HALF, R), f32),
            pltpu.VMEM((n, 2, HALF, R), bf16),
            pltpu.VMEM((n, HALF, R), bf16),
            pltpu.VMEM((n, NX, HALF, R), bf16),
            pltpu.VMEM((n, 2, HALF, R), bf16),
            pltpu.VMEM((NZ, 2, HALF, R), bf16),
            pltpu.VMEM((NZ, HALF, R), bf16),
            pltpu.VMEM((n, NY, 8, R), f32),
            pltpu.VMEM((n, NZ, 8, R), f32),
            pltpu.VMEM((n, 8, R), f32),
            dma((LOADS,)), dma(()),
            dma((2, 4)), dma((2, 4)),
            dma((NY,)), dma((NY,)),
            dma((NZ,)), dma((NZ,)),
            dma((2, NY)), dma((n, 2, NY)),
            dma((2, NZ)), dma((n, 2, NZ)),
            dma((2, NY)), dma((n, 2, NY)),
            dma(()), dma((n,)),
            dma((NX,)), dma((n, NX)),
            dma(()), dma((n,)),
            dma((NZ,)), dma((NZ,)),
            dma((NX,)), dma((n, NX)),
            dma(()), dma((n,)),
            dma((NZ,)), dma((NZ,)),
            dma(()), dma(()),
            dma((NY,)), dma((n, NY)),
            dma((NZ,)), dma((n, NZ)),
        ],
        compiler_params=pltpu.CompilerParams(
            collective_id=0, has_side_effects=True, vmem_limit_bytes=56 << 20
        ),
        cost_estimate=pl.CostEstimate(
            flops=12 * ROWS * COLS * R, bytes_accessed=2 * ROWS * COLS, transcendentals=0
        ),
    )(block, q)


def finish_kernel(m, left, right, scale, m_out, u_out, q_out):
    correction = lax.dot_general(
        left[...], right[...], (((1,), (1,)), ((), ())), preferred_element_type=f32
    )
    m_out[...] = (m[...].astype(f32) - (1.0 - momentum_decay) * correction).astype(bf16)
    u_out[...] = math.sqrt(D) * left[...].astype(f32)

    @pl.when(pl.program_id(0) == 0)
    def _():
        q_out[...] = (right[...].astype(f32) * scale[0:1, :]).astype(bf16)


def finish(block, left, right, scale):
    steps = 2
    rows = ROWS // steps
    return pl.pallas_call(
        finish_kernel,
        grid=(steps,),
        out_shape=[
            jax.ShapeDtypeStruct((ROWS, COLS), bf16),
            jax.ShapeDtypeStruct((ROWS, R), f32),
            jax.ShapeDtypeStruct((COLS, R), bf16),
        ],
        in_specs=[
            pl.BlockSpec((rows, COLS), lambda i: (i, 0)),
            pl.BlockSpec((rows, R), lambda i: (i, 0)),
            pl.BlockSpec((COLS, R), lambda i: (0, 0)),
            pl.BlockSpec((8, R), lambda i: (0, 0)),
        ],
        out_specs=[
            pl.BlockSpec((rows, COLS), lambda i: (i, 0)),
            pl.BlockSpec((rows, R), lambda i: (i, 0)),
            pl.BlockSpec((COLS, R), lambda i: (0, 0)),
        ],
        compiler_params=pltpu.CompilerParams(vmem_limit_bytes=56 << 20),
        cost_estimate=pl.CostEstimate(
            flops=2 * ROWS * COLS * R, bytes_accessed=4 * ROWS * COLS, transcendentals=0
        ),
    )(block, left, right, scale)


def shards(momentum, q_prev):
    block = momentum[0]
    left, right, scale = iterate(block, q_prev)
    momentum_next, update_left, q_next = finish(block, left, right, scale)
    return momentum_next[None], update_left, q_next


def solution(mesh):
    in_specs = (P("replica", "fsdp", "tensor"), P("tensor", None))
    out_specs = (P("replica", "fsdp", "tensor"), P("fsdp", None), P("tensor", None))
    return jax.shard_map(shards, mesh=mesh, in_specs=in_specs, out_specs=out_specs, check_vma=False)
```

```python
import functools
import math

import jax
import jax.numpy as jnp
from jax import lax
from jax.experimental import pallas as pl
from jax.experimental.pallas import tpu as pltpu
from jax.sharding import PartitionSpec as P

D = 4096
FF = 14336
R = 128
ITERS = 3
NY, NZ, NX = 8, 8, 4
ROWS = 512
COLS = 1792
LY = ROWS // NY
HALF = 128
CZ = 2 * HALF
PAD = NZ * CZ
LS = LY // 2
HR = ROWS // 2
LINKS = (4, 3)
RING = (4, 3, 5, 2, 6, 1, 7)
RING_X = (2, 1, 3)
NEAR, NEAR_X = RING[::-1], RING_X[::-1]
PLACES = "ABCD"

ridge_scale = 1e-06
norm_eps = 1e-06
momentum_decay = 0.95

MESH = pl.DeviceIdType.MESH
f32, bf16 = jnp.float32, jnp.bfloat16
HIGHEST = lax.Precision.HIGHEST


def split3(w):
    high = w.astype(bf16).astype(f32)
    rest = w - high
    mid = rest.astype(bf16).astype(f32)
    return high, mid, rest - mid


def factor_inverse(work):
    size = 16
    sub = lax.broadcasted_iota(jnp.int32, (size, R), 0)
    lane = lax.broadcasted_iota(jnp.int32, (size, R), 1)
    for first in range(0, R, size):
        left, right = work[first : first + size, 0:R], work[first : first + size, R : 2 * R]
        cols = [
            jnp.broadcast_to(left[:, first + k : first + k + 1], (size, R)) for k in range(size)
        ]
        scale = jnp.zeros((size, R), f32)
        for j in range(size):
            pivot = jnp.broadcast_to(cols[j][j : j + 1, :], (size, R))
            scale = jnp.where(sub == j, lax.rsqrt(pivot), scale)
            if j < size - 1:
                ratio = jnp.where(sub > j, cols[j], 0.0) * (1.0 / pivot)
                for k in range(j + 1, size):
                    cols[k] = cols[k] - ratio * cols[k][j : j + 1, :]
                left = left - ratio * left[j : j + 1, :]
                right = right - ratio * right[j : j + 1, :]
        left = jnp.where(lane >= first, left * scale, 0.0)
        right = right * scale
        work[first : first + size, 0:R] = left
        work[first : first + size, R : 2 * R] = right
        below = first + size
        if below < R:
            ph, pm, pw = split3(jnp.concatenate([left, right], 1))
            wh, wm, ww = split3(jnp.where(lane >= below, left, 0.0))
            a = jnp.concatenate([wh, wh, wm, wm, wh, ww], 0).astype(bf16)
            b = jnp.concatenate([ph, pm, ph, pm, pw, ph], 0).astype(bf16)
            update = lax.dot_general(a, b, (((0,), (0,)), ((), ())), preferred_element_type=f32)
            work[below:R, :] = work[below:R, :] - update[below:R, :]


def iterate_kernel(
    m_hbm, q_hbm, lr_ref, rr_ref, d_ref,
    m, q, ms, ring, ls, ly, lz, p1, p2, la, gc, gx, gs, work, rcs, rc, ro, rzs, rz, r2, r2s, r2c, rx, ra, rf, rfm,
    cy, cz, column_sq, m_sem, q_sem, ring_s, ring_r, ly_s, ly_r, lz_s, lz_r, p1_s, p1_r, p2_s, p2_r, la_s, la_r, gc_s, gc_r,
    gx_s, gx_r, rc_s, rc_r, rz_s, rz_r, rx_s, rx_r, ra_s, ra_r, rf_s, rf_r, rm_s, rm_r,
    cy_s, cy_r, cz_s, cz_r,
):
    z, fs, y = lax.axis_index("replica"), lax.axis_index("fsdp"), lax.axis_index("tensor")
    x, c = fs // 2, lax.rem(fs, 2)
    mate = {"fsdp": x * 2 + 1 - c}

    def at_y(k):
        return {"tensor": lax.rem(y + k, NY)}

    def at_z(k):
        return {"replica": lax.rem(z + k, NZ)}

    def at_x(k):
        return {"fsdp": lax.rem(x + k, NX) * 2 + c}

    def copy(src, dst, send, recv, to):
        return pltpu.make_async_remote_copy(
            src_ref=src, dst_ref=dst, send_sem=send, recv_sem=recv, device_id=to, device_id_type=MESH
        )

    barrier = pltpu.get_barrier_semaphore()
    for k in RING:
        pl.semaphore_signal(barrier, inc=1, device_id=at_y(k), device_id_type=MESH)
        pl.semaphore_signal(barrier, inc=1, device_id=at_z(k), device_id_type=MESH)
    for k in RING_X:
        pl.semaphore_signal(barrier, inc=1, device_id=at_x(k), device_id_type=MESH)
    pl.semaphore_signal(barrier, inc=1, device_id=mate, device_id_type=MESH)
    load_q = pltpu.make_async_copy(q_hbm, q, q_sem)
    load_q.start()
    load_m = pltpu.make_async_copy(m_hbm, m.at[:, pl.ds(0, COLS)], m_sem)
    load_m.start()
    m[:, COLS:PAD] = jnp.zeros((ROWS, PAD - COLS), bf16)
    load_q.wait()
    load_m.wait()
    ls[0] = jnp.dot(m[:, 0:COLS], q[...], preferred_element_type=f32).astype(bf16)
    pl.semaphore_wait(barrier, NY + NZ + NX - 2)

    def chunk(j):
        return pl.ds(pl.multiple_of(lax.rem(j + 2 * NZ, NZ) * CZ, CZ), CZ)

    def ring_chunk(way, step):
        return chunk(z + 5 - step if way == 0 else z - 4 + step)

    def ring_copy(way, half, step):
        rows = pl.ds(half * HR, HR)
        src = m.at[rows, ring_chunk(way, 1)] if step == 1 else ring.at[way, half, step - 2]
        return copy(src, ring.at[way, half, step - 1], ring_s.at[way, half, step - 1],
                    ring_r.at[way, half, step - 1], at_z(1 if way == 0 else NZ - 1))

    def ring_step(step):
        for half in range(2):
            for way in range(2):
                if step <= LINKS[way]:
                    if step > 1:
                        ring_copy(way, half, step - 1).wait_recv()
                        own = m[pl.ds(half * HR, HR), ring_chunk(way, step)].astype(f32)
                        come = ring[way, half, step - 2].astype(f32)
                        ring[way, half, step - 2] = (come + own).astype(bf16)
                    ring_copy(way, half, step).start()

    def ring_end():
        for half in range(2):
            rows = slice(half * HR, (half + 1) * HR)
            total = m[rows, chunk(z)].astype(f32)
            for way in range(2):
                ring_copy(way, half, LINKS[way]).wait_recv()
                total = total + ring[way, half, LINKS[way] - 1].astype(f32)
            high = total.astype(bf16)
            ms[rows, 0:CZ] = high
            ms[rows, CZ : 2 * CZ] = (total - high.astype(f32)).astype(bf16)

    sends = []

    def start(cp):
        cp.start()
        sends.append(cp)

    def wait_sends():
        for cp in sends:
            cp.wait_send()
        sends.clear()

    def triangular(rows):
        return lax.dot_general(
            rows, work[:, R : 2 * R], (((1,), (1,)), ((), ())),
            preferred_element_type=f32, precision=HIGHEST,
        )

    def squares(it, right):
        cy[it, y] = jnp.broadcast_to(jnp.sum(right * right, axis=0, keepdims=True), (8, R))
        for k in RING:
            start(copy(cy.at[it, y], cy.at[it, y], cy_s.at[k], cy_r.at[it, y], at_y(k)))

    def squares_over_y(it):
        for k in NEAR:
            s = lax.rem(y + k, NY)
            copy(cy.at[it, s], cy.at[it, s], cy_s.at[k], cy_r.at[it, s], at_y(k)).wait_recv()
        total = cy[it, 0]
        for s in range(1, NY):
            total = total + cy[it, s]
        cz[it, z] = total
        for k in RING:
            start(copy(cz.at[it, z], cz.at[it, z], cz_s.at[k], cz_r.at[it, z], at_z(k)))

    def squares_over_z(it):
        for k in NEAR:
            s = lax.rem(z + k, NZ)
            copy(cz.at[it, s], cz.at[it, s], cz_s.at[k], cz_r.at[it, s], at_z(k)).wait_recv()
        total = cz[it, 0]
        for s in range(1, NZ):
            total = total + cz[it, s]
        column_sq[it] = total

    def column_scale(it):
        return math.sqrt(FF) / jnp.sqrt(column_sq[it] + norm_eps)

    def factorise(it):
        for k in NEAR_X:
            s = lax.rem(x + k, NX)
            copy(gx.at[it, s], gx.at[it, s], gx_s.at[k], gx_r.at[it, s], at_x(k)).wait_recv()
        gram = (gx[it, 0].astype(f32) + gx[it, 1].astype(f32)) + (
            gx[it, 2].astype(f32) + gx[it, 3].astype(f32)
        )
        if it > 0:
            scale = jnp.broadcast_to(column_scale(it - 1)[0:1, :], (R, R))
            gram = gram * scale * scale.T
        eye = lax.broadcasted_iota(jnp.int32, (R, R), 0) == lax.broadcasted_iota(
            jnp.int32, (R, R), 1
        )
        ridge = (ridge_scale / R) * jnp.sum(jnp.where(eye, gram, 0.0), keepdims=True)
        work[:, 0:R] = jnp.where(eye, gram + ridge, gram)
        work[:, R : 2 * R] = jnp.where(eye, 1.0, 0.0)
        factor_inverse(work)
        if it > 0:
            work[:, R : 2 * R] = work[:, R : 2 * R] * scale

    def right_total(it):
        return (rx[it, 0].astype(f32) + rx[it, 1].astype(f32)) + (
            rx[it, 2].astype(f32) + rx[it, 3].astype(f32)
        )

    def right_raw(it):
        return ra[it].reshape(CZ, R)

    def left_factor():
        for k in RING:
            t = lax.rem(y + k, NY)
            start(copy(ls.at[0, pl.ds(t * LY, LY)], ly.at[y], ly_s.at[k], ly_r.at[y], at_y(k)))
        ring_at(0, "A")
        total = ls[0, pl.ds(y * LY, LY), :].astype(f32)
        for k in NEAR:
            s = lax.rem(y + k, NY)
            copy(ly.at[s], ly.at[s], ly_s.at[k], ly_r.at[s], at_y(k)).wait_recv()
            total = total + ly[s].astype(f32)
        lz[z] = total.astype(bf16)
        for k in RING:
            start(copy(lz.at[z], lz.at[z], lz_s.at[k], lz_r.at[z], at_z(k)))
        ring_at(0, "B")
        for k in NEAR:
            s = lax.rem(z + k, NZ)
            copy(lz.at[s], lz.at[s], lz_s.at[k], lz_r.at[s], at_z(k)).wait_recv()
        total = lz[0].astype(f32)
        for s in range(1, NZ):
            total = total + lz[s].astype(f32)
        la[0, pl.ds(y * LY, LY), :] = (total * (1.0 / NZ)).astype(bf16)
        mine = la.at[0, pl.ds(y * LY, LY)]
        for k in RING:
            start(copy(mine, mine, la_s.at[0, k], la_r.at[0, 0, y], at_y(k)))
        ring_at(0, "C")
        for k in NEAR:
            s = lax.rem(y + k, NY)
            theirs = la.at[0, pl.ds(s * LY, LY)]
            copy(theirs, theirs, la_s.at[0, k], la_r.at[0, 0, s], at_y(k)).wait_recv()

    def left_halves(it):
        there = ra.at[it - 1, 1 - c]
        copy(there, there, ra_s, ra_r.at[it - 1], mate).wait_recv()
        rows = right_raw(it - 1)
        ls[it] = jnp.dot(
            ms[...], jnp.concatenate([rows, rows], 0), preferred_element_type=f32
        ).astype(bf16)

        def ours(half, k):
            return pl.ds(lax.rem((z if half else y) + k, NZ) * LS + half * (ROWS // 2), LS)

        def other(half, k):
            return at_z(k) if half else at_y(k)

        me = (y, z)
        for k in RING:
            for half in range(2):
                start(copy(ls.at[it, ours(half, k)], p1.at[it, half, me[half]],
                           p1_s.at[half, k], p1_r.at[it, half, me[half]], other(half, k)))
        factorise(it - 1)
        squares(it - 1, triangular(right_raw(it - 1).astype(f32)) * (1.0 / NZ))
        totals = [ls[it, ours(half, 0), :].astype(f32) for half in range(2)]
        for k in NEAR:
            for half in range(2):
                s = lax.rem(me[half] + k, NZ)
                there = p1.at[it, half, s]
                copy(there, there, p1_s.at[half, k], p1_r.at[it, half, s], other(half, k)).wait_recv()
                totals[half] = totals[half] + p1[it, half, s].astype(f32)
        for half in range(2):
            p2[it, half, me[1 - half]] = totals[half].astype(bf16)
        for k in RING:
            for half in range(2):
                mine = p2.at[it, half, me[1 - half]]
                start(copy(mine, mine, p2_s.at[half, k], p2_r.at[it, half, me[1 - half]],
                           other(1 - half, k)))
        squares_over_y(it - 1)
        for k in NEAR:
            for half in range(2):
                s = lax.rem(me[1 - half] + k, NZ)
                there = p2.at[it, half, s]
                copy(there, there, p2_s.at[half, k], p2_r.at[it, half, s], other(1 - half, k)).wait_recv()
        totals = []
        for half in range(2):
            total = p2[it, half, 0].astype(f32)
            for s in range(1, NZ):
                total = total + p2[it, half, s].astype(f32)
            totals.append(total)
        total = triangular(jnp.concatenate(totals, 0)) * (1.0 / NZ**2)
        for half in range(2):
            la[it, ours(half, 0), :] = total[half * LS : (half + 1) * LS, :].astype(bf16)
        for k in RING:
            for half in range(2):
                mine = la.at[it, ours(half, 0)]
                start(copy(mine, mine, la_s.at[half, k], la_r.at[it, half, me[half]], other(half, k)))
        squares_over_z(it - 1)
        for k in NEAR:
            for half in range(2):
                theirs = la.at[it, ours(half, k)]
                s = lax.rem(me[half] + k, NZ)
                copy(theirs, theirs, la_s.at[half, k], la_r.at[it, half, s], other(half, k)).wait_recv()

    def ring_at(it, point):
        if it == 0 and point in PLACES:
            ring_step(PLACES.index(point) + 1)

    def right_factor(it):
        left = la[it]
        gs[it] = lax.dot_general(left, left, (((0,), (0,)), ((), ())), preferred_element_type=f32)
        start(copy(gs.at[it], gc.at[it], gc_s, gc_r.at[it], mate))
        if it == 0:
            ro[...] = (
                lax.dot_general(m[...], left, (((0,), (0,)), ((), ())), preferred_element_type=f32)
                .reshape(NZ, 2, HALF, R)
            )
            rcs[...] = ro[:, 1 - c].astype(bf16)
            to_mate = copy(rcs, rc, rc_s, rc_r.at[it], mate)
        else:
            both = lax.dot_general(ms[...], left, (((0,), (0,)), ((), ())), preferred_element_type=f32)
            both = (both[0:CZ, :] + both[CZ : 2 * CZ, :]).reshape(2, HALF, R)
            r2[...] = both
            r2s[it] = both.astype(bf16)
            to_mate = copy(r2s.at[it, 1 - c], r2c.at[it], rc_s, rc_r.at[it], mate)
        start(to_mate)
        copy(gs.at[it], gc.at[it], gc_s, gc_r.at[it], mate).wait_recv()
        gx[it, x] = (gs[it] + gc[it]).astype(bf16)
        for k in RING_X:
            start(copy(gx.at[it, x], gx.at[it, x], gx_s.at[k], gx_r.at[it, x], at_x(k)))
        to_mate.wait_recv()
        if it == 0:
            rzs[...] = (ro[:, c] + rc[...].astype(f32)).astype(bf16)
            for k in RING:
                t = lax.rem(z + k, NZ)
                start(copy(rzs.at[t], rz.at[z], rz_s.at[k], rz_r.at[z], at_z(k)))
            ring_at(it, "D")
            total = rzs[z].astype(f32)
            for k in NEAR:
                s = lax.rem(z + k, NZ)
                copy(rz.at[s], rz.at[s], rz_s.at[k], rz_r.at[s], at_z(k)).wait_recv()
                total = total + rz[s].astype(f32)
        else:
            total = r2[c] + r2c[it].astype(f32)
        rx[it, x] = total.astype(bf16)
        for k in RING_X:
            start(copy(rx.at[it, x], rx.at[it, x], rx_s.at[k], rx_r.at[it, x], at_x(k)))
        ring_at(it, "E")
        for k in NEAR_X:
            s = lax.rem(x + k, NX)
            copy(rx.at[it, s], rx.at[it, s], rx_s.at[k], rx_r.at[it, s], at_x(k)).wait_recv()

    last = ITERS - 1
    for it in range(ITERS):
        if it == 0:
            left_factor()
        else:
            left_halves(it)
        right_factor(it)
        ra[it, c] = right_total(it).astype(bf16)
        to_mate = copy(ra.at[it, c], ra.at[it, c], ra_s, ra_r.at[it], mate)
        to_mate.start()
        if it == 0:
            ring_end()
        wait_sends()
        sends.append(to_mate)

    factorise(last)
    there = ra.at[last, 1 - c]
    copy(there, there, ra_s, ra_r.at[last], mate).wait_recv()
    right = triangular(right_raw(last).astype(f32)) * (1.0 / NZ)
    squares(last, right)
    rf[z] = right.astype(bf16).reshape(2, HALF, R)
    mine = rf.at[z, c]
    for k in RING:
        start(copy(mine, mine, rf_s.at[k], rf_r.at[z], at_z(k)))
    lr_ref[...] = triangular(la[last].astype(f32)).astype(bf16)
    squares_over_y(last)
    for k in NEAR:
        s = lax.rem(z + k, NZ)
        there = rf.at[s, c]
        copy(there, there, rf_s.at[k], rf_r.at[s], at_z(k)).wait_recv()
    start(copy(rf.at[:, c], rfm, rm_s, rm_r, mate))
    squares_over_z(last)
    copy(rfm, rfm, rm_s, rm_r, mate).wait_recv()
    for k in range(COLS // CZ):
        rr_ref[pl.ds(k * CZ + c * HALF, HALF), :] = rf[k, c]
        rr_ref[pl.ds(k * CZ + (1 - c) * HALF, HALF), :] = rfm[k]
    d_ref[...] = column_scale(last)
    wait_sends()
    for way in range(2):
        for half in range(2):
            for step in range(1, LINKS[way] + 1):
                ring_copy(way, half, step).wait_send()


def iterate(block, q):
    vmem = pl.BlockSpec(memory_space=pltpu.VMEM)
    hbm = pl.BlockSpec(memory_space=pltpu.HBM)
    dma = pltpu.SemaphoreType.DMA
    n = ITERS
    return pl.pallas_call(
        iterate_kernel,
        out_shape=[
            jax.ShapeDtypeStruct((ROWS, R), bf16),
            jax.ShapeDtypeStruct((COLS, R), bf16),
            jax.ShapeDtypeStruct((8, R), f32),
        ],
        in_specs=[hbm, hbm],
        out_specs=[vmem] * 3,
        scratch_shapes=[
            pltpu.VMEM((ROWS, PAD), bf16),
            pltpu.VMEM((COLS, R), bf16),
            pltpu.VMEM((ROWS, 2 * CZ), bf16),
            pltpu.VMEM((2, 2, 4, HR, CZ), bf16),
            pltpu.VMEM((n, ROWS, R), bf16),
            pltpu.VMEM((NY, LY, R), bf16),
            pltpu.VMEM((NZ, LY, R), bf16),
            pltpu.VMEM((n, 2, NY, LS, R), bf16),
            pltpu.VMEM((n, 2, NZ, LS, R), bf16),
            pltpu.VMEM((n, ROWS, R), bf16),
            pltpu.VMEM((n, R, R), f32),
            pltpu.VMEM((n, NX, R, R), bf16),
            pltpu.VMEM((n, R, R), f32),
            pltpu.VMEM((R, 2 * R), f32),
            pltpu.VMEM((NZ, HALF, R), bf16),
            pltpu.VMEM((NZ, HALF, R), bf16),
            pltpu.VMEM((NZ, 2, HALF, R), f32),
            pltpu.VMEM((NZ, HALF, R), bf16),
            pltpu.VMEM((NZ, HALF, R), bf16),
            pltpu.VMEM((2, HALF, R), f32),
            pltpu.VMEM((n, 2, HALF, R), bf16),
            pltpu.VMEM((n, HALF, R), bf16),
            pltpu.VMEM((n, NX, HALF, R), bf16),
            pltpu.VMEM((n, 2, HALF, R), bf16),
            pltpu.VMEM((NZ, 2, HALF, R), bf16),
            pltpu.VMEM((NZ, HALF, R), bf16),
            pltpu.VMEM((n, NY, 8, R), f32),
            pltpu.VMEM((n, NZ, 8, R), f32),
            pltpu.VMEM((n, 8, R), f32),
            dma(()), dma(()),
            dma((2, 2, 4)), dma((2, 2, 4)),
            dma((NY,)), dma((NY,)),
            dma((NZ,)), dma((NZ,)),
            dma((2, NY)), dma((n, 2, NY)),
            dma((2, NZ)), dma((n, 2, NZ)),
            dma((2, NY)), dma((n, 2, NY)),
            dma(()), dma((n,)),
            dma((NX,)), dma((n, NX)),
            dma(()), dma((n,)),
            dma((NZ,)), dma((NZ,)),
            dma((NX,)), dma((n, NX)),
            dma(()), dma((n,)),
            dma((NZ,)), dma((NZ,)),
            dma(()), dma(()),
            dma((NY,)), dma((n, NY)),
            dma((NZ,)), dma((n, NZ)),
        ],
        compiler_params=pltpu.CompilerParams(
            collective_id=0, has_side_effects=True, vmem_limit_bytes=56 << 20
        ),
        cost_estimate=pl.CostEstimate(
            flops=12 * ROWS * COLS * R, bytes_accessed=2 * ROWS * COLS, transcendentals=0
        ),
    )(block, q)


def finish_kernel(m, left, right, scale, m_out, u_out, q_out):
    correction = lax.dot_general(
        left[...], right[...], (((1,), (1,)), ((), ())), preferred_element_type=f32
    )
    m_out[...] = (m[...].astype(f32) - (1.0 - momentum_decay) * correction).astype(bf16)
    u_out[...] = math.sqrt(D) * left[...].astype(f32)

    @pl.when(pl.program_id(0) == 0)
    def _():
        q_out[...] = (right[...].astype(f32) * scale[0:1, :]).astype(bf16)


def finish(block, left, right, scale):
    steps = 2
    rows = ROWS // steps
    return pl.pallas_call(
        finish_kernel,
        grid=(steps,),
        out_shape=[
            jax.ShapeDtypeStruct((ROWS, COLS), bf16),
            jax.ShapeDtypeStruct((ROWS, R), f32),
            jax.ShapeDtypeStruct((COLS, R), bf16),
        ],
        in_specs=[
            pl.BlockSpec((rows, COLS), lambda i: (i, 0)),
            pl.BlockSpec((rows, R), lambda i: (i, 0)),
            pl.BlockSpec((COLS, R), lambda i: (0, 0)),
            pl.BlockSpec((8, R), lambda i: (0, 0)),
        ],
        out_specs=[
            pl.BlockSpec((rows, COLS), lambda i: (i, 0)),
            pl.BlockSpec((rows, R), lambda i: (i, 0)),
            pl.BlockSpec((COLS, R), lambda i: (0, 0)),
        ],
        compiler_params=pltpu.CompilerParams(vmem_limit_bytes=56 << 20),
        cost_estimate=pl.CostEstimate(
            flops=2 * ROWS * COLS * R, bytes_accessed=4 * ROWS * COLS, transcendentals=0
        ),
    )(block, left, right, scale)


def shards(momentum, q_prev):
    block = momentum[0]
    left, right, scale = iterate(block, q_prev)
    momentum_next, update_left, q_next = finish(block, left, right, scale)
    return momentum_next[None], update_left, q_next


def solution(mesh):
    in_specs = (P("replica", "fsdp", "tensor"), P("tensor", None))
    out_specs = (P("replica", "fsdp", "tensor"), P("fsdp", None), P("tensor", None))
    return jax.shard_map(shards, mesh=mesh, in_specs=in_specs, out_specs=out_specs, check_vma=False)
```

```python
import functools
import math

import jax
import jax.numpy as jnp
from jax import lax
from jax.experimental import pallas as pl
from jax.experimental.pallas import tpu as pltpu
from jax.sharding import PartitionSpec as P

D = 4096
FF = 14336
R = 128
ITERS = 3
NY, NZ, NX = 8, 8, 4
ROWS = 512
COLS = 1792
LY = ROWS // NY
HALF = 128
CZ = 2 * HALF
PAD = NZ * CZ
LS = LY // 2
HR = ROWS // 2
LINKS = (4, 3)
RING = (4, 3, 5, 2, 6, 1, 7)
RING_X = (2, 1, 3)
NEAR, NEAR_X = RING[::-1], RING_X[::-1]
PLACES = "ABCD"

ridge_scale = 1e-06
norm_eps = 1e-06
momentum_decay = 0.95

MESH = pl.DeviceIdType.MESH
f32, bf16 = jnp.float32, jnp.bfloat16
HIGHEST = lax.Precision.HIGHEST


def split3(w):
    high = w.astype(bf16).astype(f32)
    rest = w - high
    mid = rest.astype(bf16).astype(f32)
    return high, mid, rest - mid


def factor_inverse(work):
    size = 16
    sub = lax.broadcasted_iota(jnp.int32, (size, R), 0)
    lane = lax.broadcasted_iota(jnp.int32, (size, R), 1)
    for first in range(0, R, size):
        left, right = work[first : first + size, 0:R], work[first : first + size, R : 2 * R]
        cols = [
            jnp.broadcast_to(left[:, first + k : first + k + 1], (size, R)) for k in range(size)
        ]
        scale = jnp.zeros((size, R), f32)
        for j in range(size):
            pivot = jnp.broadcast_to(cols[j][j : j + 1, :], (size, R))
            scale = jnp.where(sub == j, lax.rsqrt(pivot), scale)
            if j < size - 1:
                ratio = jnp.where(sub > j, cols[j], 0.0) * (1.0 / pivot)
                for k in range(j + 1, size):
                    cols[k] = cols[k] - ratio * cols[k][j : j + 1, :]
                left = left - ratio * left[j : j + 1, :]
                right = right - ratio * right[j : j + 1, :]
        left = jnp.where(lane >= first, left * scale, 0.0)
        right = right * scale
        work[first : first + size, 0:R] = left
        work[first : first + size, R : 2 * R] = right
        below = first + size
        if below < R:
            ph, pm, pw = split3(jnp.concatenate([left, right], 1))
            wh, wm, ww = split3(jnp.where(lane >= below, left, 0.0))
            a = jnp.concatenate([wh, wh, wm, wm, wh, ww], 0).astype(bf16)
            b = jnp.concatenate([ph, pm, ph, pm, pw, ph], 0).astype(bf16)
            update = lax.dot_general(a, b, (((0,), (0,)), ((), ())), preferred_element_type=f32)
            work[below:R, :] = work[below:R, :] - update[below:R, :]


def iterate_kernel(
    m_hbm, q_hbm, lr_ref, rr_ref, d_ref,
    m, q, ms, ring, ls, ly, lz, p1, p2, la, gc, gx, gs, work, rcs, rc, ro, rzs, rz, r2, r2s, r2c, rx, ra, rf, rfm,
    cy, cz, column_sq, m_sem, q_sem, ring_s, ring_r, ly_s, ly_r, lz_s, lz_r, p1_s, p1_r, p2_s, p2_r, la_s, la_r, gc_s, gc_r,
    gx_s, gx_r, rc_s, rc_r, rz_s, rz_r, rx_s, rx_r, ra_s, ra_r, rf_s, rf_r, rm_s, rm_r,
    cy_s, cy_r, cz_s, cz_r,
):
    z, fs, y = lax.axis_index("replica"), lax.axis_index("fsdp"), lax.axis_index("tensor")
    x, c = fs // 2, lax.rem(fs, 2)
    mate = {"fsdp": x * 2 + 1 - c}

    def at_y(k):
        return {"tensor": lax.rem(y + k, NY)}

    def at_z(k):
        return {"replica": lax.rem(z + k, NZ)}

    def at_x(k):
        return {"fsdp": lax.rem(x + k, NX) * 2 + c}

    def copy(src, dst, send, recv, to):
        return pltpu.make_async_remote_copy(
            src_ref=src, dst_ref=dst, send_sem=send, recv_sem=recv, device_id=to, device_id_type=MESH
        )

    barrier = pltpu.get_barrier_semaphore()
    for k in RING:
        pl.semaphore_signal(barrier, inc=1, device_id=at_y(k), device_id_type=MESH)
        pl.semaphore_signal(barrier, inc=1, device_id=at_z(k), device_id_type=MESH)
    for k in RING_X:
        pl.semaphore_signal(barrier, inc=1, device_id=at_x(k), device_id_type=MESH)
    pl.semaphore_signal(barrier, inc=1, device_id=mate, device_id_type=MESH)
    load_q = pltpu.make_async_copy(q_hbm, q, q_sem)
    load_q.start()
    load_m = pltpu.make_async_copy(m_hbm, m.at[:, pl.ds(0, COLS)], m_sem)
    load_m.start()
    m[:, COLS:PAD] = jnp.zeros((ROWS, PAD - COLS), bf16)
    load_q.wait()
    load_m.wait()
    ls[0] = jnp.dot(m[:, 0:COLS], q[...], preferred_element_type=f32).astype(bf16)
    pl.semaphore_wait(barrier, NY + NZ + NX - 2)

    def chunk(j):
        return pl.ds(pl.multiple_of(lax.rem(j + 2 * NZ, NZ) * CZ, CZ), CZ)

    def ring_chunk(way, step):
        return chunk(z + 5 - step if way == 0 else z - 4 + step)

    def ring_copy(way, half, step):
        rows = pl.ds(half * HR, HR)
        src = m.at[rows, ring_chunk(way, 1)] if step == 1 else ring.at[way, half, step - 2]
        return copy(src, ring.at[way, half, step - 1], ring_s.at[way, half, step - 1],
                    ring_r.at[way, half, step - 1], at_z(1 if way == 0 else NZ - 1))

    def ring_step(step):
        for half in range(2):
            for way in range(2):
                if step <= LINKS[way]:
                    if step > 1:
                        ring_copy(way, half, step - 1).wait_recv()
                        own = m[pl.ds(half * HR, HR), ring_chunk(way, step)].astype(f32)
                        come = ring[way, half, step - 2].astype(f32)
                        ring[way, half, step - 2] = (come + own).astype(bf16)
                    ring_copy(way, half, step).start()

    def ring_end():
        for half in range(2):
            rows = slice(half * HR, (half + 1) * HR)
            total = m[rows, chunk(z)].astype(f32)
            for way in range(2):
                ring_copy(way, half, LINKS[way]).wait_recv()
                total = total + ring[way, half, LINKS[way] - 1].astype(f32)
            high = total.astype(bf16)
            ms[rows, 0:CZ] = high
            ms[rows, CZ : 2 * CZ] = (total - high.astype(f32)).astype(bf16)

    sends = []

    def start(cp):
        cp.start()
        sends.append(cp)

    def wait_sends():
        for cp in sends:
            cp.wait_send()
        sends.clear()

    def triangular(rows):
        return lax.dot_general(
            rows, work[:, R : 2 * R], (((1,), (1,)), ((), ())),
            preferred_element_type=f32, precision=HIGHEST,
        )

    def squares(it, right):
        cy[it, y] = jnp.broadcast_to(jnp.sum(right * right, axis=0, keepdims=True), (8, R))
        for k in RING:
            start(copy(cy.at[it, y], cy.at[it, y], cy_s.at[k], cy_r.at[it, y], at_y(k)))

    def squares_over_y(it):
        for k in NEAR:
            s = lax.rem(y + k, NY)
            copy(cy.at[it, s], cy.at[it, s], cy_s.at[k], cy_r.at[it, s], at_y(k)).wait_recv()
        total = cy[it, 0]
        for s in range(1, NY):
            total = total + cy[it, s]
        cz[it, z] = total
        for k in RING:
            start(copy(cz.at[it, z], cz.at[it, z], cz_s.at[k], cz_r.at[it, z], at_z(k)))

    def squares_over_z(it):
        for k in NEAR:
            s = lax.rem(z + k, NZ)
            copy(cz.at[it, s], cz.at[it, s], cz_s.at[k], cz_r.at[it, s], at_z(k)).wait_recv()
        total = cz[it, 0]
        for s in range(1, NZ):
            total = total + cz[it, s]
        column_sq[it] = total

    def column_scale(it):
        return math.sqrt(FF) / jnp.sqrt(column_sq[it] + norm_eps)

    def factorise(it):
        if it > 0:
            scale = jnp.broadcast_to(column_scale(it - 1)[0:1, :], (R, R))
            scales = scale * scale.T
        for k in NEAR_X:
            s = lax.rem(x + k, NX)
            copy(gx.at[it, s], gx.at[it, s], gx_s.at[k], gx_r.at[it, s], at_x(k)).wait_recv()
        gram = (gx[it, 0].astype(f32) + gx[it, 1].astype(f32)) + (
            gx[it, 2].astype(f32) + gx[it, 3].astype(f32)
        )
        if it > 0:
            gram = gram * scales
        eye = lax.broadcasted_iota(jnp.int32, (R, R), 0) == lax.broadcasted_iota(
            jnp.int32, (R, R), 1
        )
        ridge = (ridge_scale / R) * jnp.sum(jnp.where(eye, gram, 0.0), keepdims=True)
        work[:, 0:R] = jnp.where(eye, gram + ridge, gram)
        work[:, R : 2 * R] = jnp.where(eye, 1.0, 0.0)
        factor_inverse(work)
        if it > 0:
            work[:, R : 2 * R] = work[:, R : 2 * R] * scale

    def right_total(it):
        return (rx[it, 0].astype(f32) + rx[it, 1].astype(f32)) + (
            rx[it, 2].astype(f32) + rx[it, 3].astype(f32)
        )

    def right_raw(it):
        return ra[it].reshape(CZ, R)

    def left_factor():
        for k in RING:
            t = lax.rem(y + k, NY)
            start(copy(ls.at[0, pl.ds(t * LY, LY)], ly.at[y], ly_s.at[k], ly_r.at[y], at_y(k)))
        ring_at(0, "A")
        total = ls[0, pl.ds(y * LY, LY), :].astype(f32)
        for k in NEAR:
            s = lax.rem(y + k, NY)
            copy(ly.at[s], ly.at[s], ly_s.at[k], ly_r.at[s], at_y(k)).wait_recv()
            total = total + ly[s].astype(f32)
        lz[z] = total.astype(bf16)
        for k in RING:
            start(copy(lz.at[z], lz.at[z], lz_s.at[k], lz_r.at[z], at_z(k)))
        ring_at(0, "B")
        for k in NEAR:
            s = lax.rem(z + k, NZ)
            copy(lz.at[s], lz.at[s], lz_s.at[k], lz_r.at[s], at_z(k)).wait_recv()
        total = lz[0].astype(f32)
        for s in range(1, NZ):
            total = total + lz[s].astype(f32)
        la[0, pl.ds(y * LY, LY), :] = (total * (1.0 / NZ)).astype(bf16)
        mine = la.at[0, pl.ds(y * LY, LY)]
        for k in RING:
            start(copy(mine, mine, la_s.at[0, k], la_r.at[0, 0, y], at_y(k)))
        ring_at(0, "C")
        for k in NEAR:
            s = lax.rem(y + k, NY)
            theirs = la.at[0, pl.ds(s * LY, LY)]
            copy(theirs, theirs, la_s.at[0, k], la_r.at[0, 0, s], at_y(k)).wait_recv()

    def left_halves(it):
        there = ra.at[it - 1, 1 - c]
        copy(there, there, ra_s, ra_r.at[it - 1], mate).wait_recv()
        rows = right_raw(it - 1)
        ls[it] = jnp.dot(
            ms[...], jnp.concatenate([rows, rows], 0), preferred_element_type=f32
        ).astype(bf16)

        def ours(half, k):
            return pl.ds(lax.rem((z if half else y) + k, NZ) * LS + half * (ROWS // 2), LS)

        def other(half, k):
            return at_z(k) if half else at_y(k)

        me = (y, z)
        for k in RING:
            for half in range(2):
                start(copy(ls.at[it, ours(half, k)], p1.at[it, half, me[half]],
                           p1_s.at[half, k], p1_r.at[it, half, me[half]], other(half, k)))
        factorise(it - 1)
        squares(it - 1, triangular(right_raw(it - 1).astype(f32)) * (1.0 / NZ))
        totals = [ls[it, ours(half, 0), :].astype(f32) for half in range(2)]
        for k in NEAR:
            for half in range(2):
                s = lax.rem(me[half] + k, NZ)
                there = p1.at[it, half, s]
                copy(there, there, p1_s.at[half, k], p1_r.at[it, half, s], other(half, k)).wait_recv()
                totals[half] = totals[half] + p1[it, half, s].astype(f32)
        for half in range(2):
            p2[it, half, me[1 - half]] = totals[half].astype(bf16)
        for k in RING:
            for half in range(2):
                mine = p2.at[it, half, me[1 - half]]
                start(copy(mine, mine, p2_s.at[half, k], p2_r.at[it, half, me[1 - half]],
                           other(1 - half, k)))
        squares_over_y(it - 1)
        for k in NEAR:
            for half in range(2):
                s = lax.rem(me[1 - half] + k, NZ)
                there = p2.at[it, half, s]
                copy(there, there, p2_s.at[half, k], p2_r.at[it, half, s], other(1 - half, k)).wait_recv()
        totals = []
        for half in range(2):
            total = p2[it, half, 0].astype(f32)
            for s in range(1, NZ):
                total = total + p2[it, half, s].astype(f32)
            totals.append(total)
        total = triangular(jnp.concatenate(totals, 0)) * (1.0 / NZ**2)
        for half in range(2):
            la[it, ours(half, 0), :] = total[half * LS : (half + 1) * LS, :].astype(bf16)
        for k in RING:
            for half in range(2):
                mine = la.at[it, ours(half, 0)]
                start(copy(mine, mine, la_s.at[half, k], la_r.at[it, half, me[half]], other(half, k)))
        squares_over_z(it - 1)
        for k in NEAR:
            for half in range(2):
                theirs = la.at[it, ours(half, k)]
                s = lax.rem(me[half] + k, NZ)
                copy(theirs, theirs, la_s.at[half, k], la_r.at[it, half, s], other(half, k)).wait_recv()

    def ring_at(it, point):
        if it == 0 and point in PLACES:
            ring_step(PLACES.index(point) + 1)

    def right_factor(it):
        left = la[it]
        gs[it] = lax.dot_general(left, left, (((0,), (0,)), ((), ())), preferred_element_type=f32)
        start(copy(gs.at[it], gc.at[it], gc_s, gc_r.at[it], mate))
        if it == 0:
            to_mate = []
            for k in range(2):
                chips, columns = slice(k * 4, k * 4 + 4), slice(k * 4 * CZ, (k * 4 + 4) * CZ)
                ro[chips] = lax.dot_general(
                    m[:, columns], left, (((0,), (0,)), ((), ())), preferred_element_type=f32
                ).reshape(4, 2, HALF, R)
                rcs[chips] = ro[chips, 1 - c].astype(bf16)
                part = pl.ds(k * 4, 4)
                to_mate.append(copy(rcs.at[part], rc.at[part], rc_s.at[k], rc_r.at[it, k], mate))
                start(to_mate[k])
        else:
            both = lax.dot_general(ms[...], left, (((0,), (0,)), ((), ())), preferred_element_type=f32)
            both = (both[0:CZ, :] + both[CZ : 2 * CZ, :]).reshape(2, HALF, R)
            r2[...] = both
            r2s[it] = both.astype(bf16)
            to_mate = [copy(r2s.at[it, 1 - c], r2c.at[it], rc_s.at[0], rc_r.at[it, 0], mate)]
            start(to_mate[0])
        copy(gs.at[it], gc.at[it], gc_s, gc_r.at[it], mate).wait_recv()
        gx[it, x] = (gs[it] + gc[it]).astype(bf16)
        for k in RING_X:
            start(copy(gx.at[it, x], gx.at[it, x], gx_s.at[k], gx_r.at[it, x], at_x(k)))
        for cp in to_mate:
            cp.wait_recv()
        if it == 0:
            rzs[...] = (ro[:, c] + rc[...].astype(f32)).astype(bf16)
            for k in RING:
                t = lax.rem(z + k, NZ)
                start(copy(rzs.at[t], rz.at[z], rz_s.at[k], rz_r.at[z], at_z(k)))
            ring_at(it, "D")
            total = rzs[z].astype(f32)
            for k in NEAR:
                s = lax.rem(z + k, NZ)
                copy(rz.at[s], rz.at[s], rz_s.at[k], rz_r.at[s], at_z(k)).wait_recv()
                total = total + rz[s].astype(f32)
        else:
            total = r2[c] + r2c[it].astype(f32)
        rx[it, x] = total.astype(bf16)
        for k in RING_X:
            start(copy(rx.at[it, x], rx.at[it, x], rx_s.at[k], rx_r.at[it, x], at_x(k)))
        ring_at(it, "E")
        for k in NEAR_X:
            s = lax.rem(x + k, NX)
            copy(rx.at[it, s], rx.at[it, s], rx_s.at[k], rx_r.at[it, s], at_x(k)).wait_recv()

    last = ITERS - 1
    for it in range(ITERS):
        if it == 0:
            left_factor()
        else:
            left_halves(it)
        right_factor(it)
        ra[it, c] = right_total(it).astype(bf16)
        to_mate = copy(ra.at[it, c], ra.at[it, c], ra_s, ra_r.at[it], mate)
        to_mate.start()
        if it == 0:
            ring_end()
        wait_sends()
        sends.append(to_mate)

    factorise(last)
    there = ra.at[last, 1 - c]
    copy(there, there, ra_s, ra_r.at[last], mate).wait_recv()
    right = triangular(right_raw(last).astype(f32)) * (1.0 / NZ)
    squares(last, right)
    rf[z] = right.astype(bf16).reshape(2, HALF, R)
    mine = rf.at[z, c]
    for k in RING:
        start(copy(mine, mine, rf_s.at[k], rf_r.at[z], at_z(k)))
    lr_ref[...] = triangular(la[last].astype(f32)).astype(bf16)
    squares_over_y(last)
    for k in NEAR:
        s = lax.rem(z + k, NZ)
        there = rf.at[s, c]
        copy(there, there, rf_s.at[k], rf_r.at[s], at_z(k)).wait_recv()
    start(copy(rf.at[:, c], rfm, rm_s, rm_r, mate))
    squares_over_z(last)
    copy(rfm, rfm, rm_s, rm_r, mate).wait_recv()
    for k in range(COLS // CZ):
        rr_ref[pl.ds(k * CZ + c * HALF, HALF), :] = rf[k, c]
        rr_ref[pl.ds(k * CZ + (1 - c) * HALF, HALF), :] = rfm[k]
    d_ref[...] = column_scale(last)
    wait_sends()
    for way in range(2):
        for half in range(2):
            for step in range(1, LINKS[way] + 1):
                ring_copy(way, half, step).wait_send()


def iterate(block, q):
    vmem = pl.BlockSpec(memory_space=pltpu.VMEM)
    hbm = pl.BlockSpec(memory_space=pltpu.HBM)
    dma = pltpu.SemaphoreType.DMA
    n = ITERS
    return pl.pallas_call(
        iterate_kernel,
        out_shape=[
            jax.ShapeDtypeStruct((ROWS, R), bf16),
            jax.ShapeDtypeStruct((COLS, R), bf16),
            jax.ShapeDtypeStruct((8, R), f32),
        ],
        in_specs=[hbm, hbm],
        out_specs=[vmem] * 3,
        scratch_shapes=[
            pltpu.VMEM((ROWS, PAD), bf16),
            pltpu.VMEM((COLS, R), bf16),
            pltpu.VMEM((ROWS, 2 * CZ), bf16),
            pltpu.VMEM((2, 2, 4, HR, CZ), bf16),
            pltpu.VMEM((n, ROWS, R), bf16),
            pltpu.VMEM((NY, LY, R), bf16),
            pltpu.VMEM((NZ, LY, R), bf16),
            pltpu.VMEM((n, 2, NY, LS, R), bf16),
            pltpu.VMEM((n, 2, NZ, LS, R), bf16),
            pltpu.VMEM((n, ROWS, R), bf16),
            pltpu.VMEM((n, R, R), f32),
            pltpu.VMEM((n, NX, R, R), bf16),
            pltpu.VMEM((n, R, R), f32),
            pltpu.VMEM((R, 2 * R), f32),
            pltpu.VMEM((NZ, HALF, R), bf16),
            pltpu.VMEM((NZ, HALF, R), bf16),
            pltpu.VMEM((NZ, 2, HALF, R), f32),
            pltpu.VMEM((NZ, HALF, R), bf16),
            pltpu.VMEM((NZ, HALF, R), bf16),
            pltpu.VMEM((2, HALF, R), f32),
            pltpu.VMEM((n, 2, HALF, R), bf16),
            pltpu.VMEM((n, HALF, R), bf16),
            pltpu.VMEM((n, NX, HALF, R), bf16),
            pltpu.VMEM((n, 2, HALF, R), bf16),
            pltpu.VMEM((NZ, 2, HALF, R), bf16),
            pltpu.VMEM((NZ, HALF, R), bf16),
            pltpu.VMEM((n, NY, 8, R), f32),
            pltpu.VMEM((n, NZ, 8, R), f32),
            pltpu.VMEM((n, 8, R), f32),
            dma(()), dma(()),
            dma((2, 2, 4)), dma((2, 2, 4)),
            dma((NY,)), dma((NY,)),
            dma((NZ,)), dma((NZ,)),
            dma((2, NY)), dma((n, 2, NY)),
            dma((2, NZ)), dma((n, 2, NZ)),
            dma((2, NY)), dma((n, 2, NY)),
            dma(()), dma((n,)),
            dma((NX,)), dma((n, NX)),
            dma((2,)), dma((n, 2)),
            dma((NZ,)), dma((NZ,)),
            dma((NX,)), dma((n, NX)),
            dma(()), dma((n,)),
            dma((NZ,)), dma((NZ,)),
            dma(()), dma(()),
            dma((NY,)), dma((n, NY)),
            dma((NZ,)), dma((n, NZ)),
        ],
        compiler_params=pltpu.CompilerParams(
            collective_id=0, has_side_effects=True, vmem_limit_bytes=56 << 20
        ),
        cost_estimate=pl.CostEstimate(
            flops=12 * ROWS * COLS * R, bytes_accessed=2 * ROWS * COLS, transcendentals=0
        ),
    )(block, q)


def finish_kernel(m, left, right, scale, m_out, u_out, q_out):
    correction = lax.dot_general(
        left[...], right[...], (((1,), (1,)), ((), ())), preferred_element_type=f32
    )
    m_out[...] = (m[...].astype(f32) - (1.0 - momentum_decay) * correction).astype(bf16)
    u_out[...] = math.sqrt(D) * left[...].astype(f32)

    @pl.when(pl.program_id(0) == 0)
    def _():
        q_out[...] = (right[...].astype(f32) * scale[0:1, :]).astype(bf16)


def finish(block, left, right, scale):
    steps = 2
    rows = ROWS // steps
    return pl.pallas_call(
        finish_kernel,
        grid=(steps,),
        out_shape=[
            jax.ShapeDtypeStruct((ROWS, COLS), bf16),
            jax.ShapeDtypeStruct((ROWS, R), f32),
            jax.ShapeDtypeStruct((COLS, R), bf16),
        ],
        in_specs=[
            pl.BlockSpec((rows, COLS), lambda i: (i, 0)),
            pl.BlockSpec((rows, R), lambda i: (i, 0)),
            pl.BlockSpec((COLS, R), lambda i: (0, 0)),
            pl.BlockSpec((8, R), lambda i: (0, 0)),
        ],
        out_specs=[
            pl.BlockSpec((rows, COLS), lambda i: (i, 0)),
            pl.BlockSpec((rows, R), lambda i: (i, 0)),
            pl.BlockSpec((COLS, R), lambda i: (0, 0)),
        ],
        compiler_params=pltpu.CompilerParams(vmem_limit_bytes=56 << 20),
        cost_estimate=pl.CostEstimate(
            flops=2 * ROWS * COLS * R, bytes_accessed=4 * ROWS * COLS, transcendentals=0
        ),
    )(block, left, right, scale)


def shards(momentum, q_prev):
    block = momentum[0]
    left, right, scale = iterate(block, q_prev)
    momentum_next, update_left, q_next = finish(block, left, right, scale)
    return momentum_next[None], update_left, q_next


def solution(mesh):
    in_specs = (P("replica", "fsdp", "tensor"), P("tensor", None))
    out_specs = (P("replica", "fsdp", "tensor"), P("fsdp", None), P("tensor", None))
    return jax.shard_map(shards, mesh=mesh, in_specs=in_specs, out_specs=out_specs, check_vma=False)
```
